512 devices in a mesh: learner: 32 (over z, y_lo), pool: 4 (over x), tp: 4 (over y_hi, core).
Axes of the slice: x: 4, y: 4 (y_hi: 2, y_lo: 2; y = y_hi * 2 + y_lo), z: 16, core: 2. Of those that a mesh axis runs over, the one named last changes fastest.
Arguments:
- gate_master: float32 [8192, 16384], P('pool', ('learner', 'tp')), may hold values from -0.0625 to 0.0625
- up_master: float32 [8192, 16384], P('pool', ('learner', 'tp')), may hold values from -0.0625 to 0.0625
- stream: float32 [2048, 8192], P(('pool', 'tp'), 'learner'), may hold values from -700 to 700
- norm_gain: float32 [8192], P('learner'), may hold values from 0.1 to 1.9
- live_rows: int32 [2048], P(('pool', 'tp')), may hold values from 0 to 1, as said below
Outputs:
- hidden: bfloat16 [2048, 16384], P('pool', ('learner', 'tp'))
The draws below stay inside these ranges and needn't reach their ends.
Inputs may be any that keep to these rules, and one draw needn't show every extreme that they name: `live_rows`: within each aligned block of 128 rows (the rows of one device) at most 64 are 1, and some block has exactly 64.
All inputs are finite; a program needn't handle non-finite values.
Results may differ from the reference program's by a relative error of at most 0.009.
Values may be sent and summed in bfloat16 or wider, within the bound.
No kernel may reach another device: no remote copies, remote signals or barrier semaphores. Data moves between devices by JAX's collectives and lax.ppermute only.
A program may use at most 64 MiB of HBM per device.

```python
import math
import jax
import jax.numpy as jnp
from jax import lax

D = 8192
FFW = 16384
BLOCK = 32
ROWS_DEV = 128
LIVE = 64
ALL_ROWS = 2048


def draw_stream(key, part):
    key = jax.random.fold_in(key, 11)
    noise_key, column_key, row_key = jax.random.split(key, 3)
    col_index = jnp.arange(D, dtype=jnp.float32)
    col_factor = 3.0 ** (col_index / D) * jnp.exp(jax.random.uniform(column_key, (D,), jnp.float32, 0.0, math.log(3.4)))
    baseline = jnp.clip(jax.random.normal(noise_key, (ALL_ROWS, D), jnp.float32), -4.0, 4.0)
    row_factor = jnp.exp(jax.random.uniform(row_key, (ALL_ROWS, 1), jnp.float32, 0.0, math.log(10.0)))
    return (baseline * row_factor * col_factor[None, :]).astype(jnp.float32)


def draw_live_rows(key, part):
    key = jax.random.fold_in(key, 23)
    count_key, fullest_key, order_key = jax.random.split(key, 3)
    blocks = ALL_ROWS // ROWS_DEV
    counts = jax.random.randint(count_key, (blocks,), 1, LIVE + 1)
    fullest = jax.random.randint(fullest_key, (), 0, blocks)
    counts = jnp.where(jnp.arange(blocks) == fullest, LIVE, counts)
    block_keys = jax.random.split(order_key, blocks)
    rank_table = jax.vmap(lambda block_key: jax.random.permutation(block_key, ROWS_DEV))(block_keys)
    return (rank_table < counts[:, None]).astype(jnp.int32).reshape(-1)


def block_levels(own_key, extent, cuts, smallest, high):
    def one(position, parts):
        steps = jax.random.uniform(jax.random.fold_in(jax.random.fold_in(own_key, 6), position), (parts,), jnp.float32, smallest / len(cuts), high / len(cuts))
        return jnp.repeat(jnp.exp(steps), extent[position] // parts).reshape((-1,) + (1,) * (len(extent) - position - 1))

    loudness = one(*cuts[0])
    for cut in cuts[1:]:
        loudness = loudness * one(*cut)
    return loudness


def noise(stream_key, dims, spread, reach, cuts=(), held_as=jnp.bfloat16):
    values = spread * jax.random.normal(stream_key, dims, jnp.float32)
    if cuts:
        values = values * block_levels(stream_key, dims, cuts, -0.22, 0.18)
    return jnp.clip(values, -reach, reach).astype(held_as)


def setup_inputs(seed: int = 0) -> dict:
    arg_keys = jax.random.split(jax.random.key(seed), 6)
    gate_master = noise(arg_keys[0], (D, FFW), D ** -0.5, 0.0625, ((0, 4), (1, 128)), jnp.float32)
    up_master = noise(arg_keys[1], (D, FFW), D ** -0.5, 0.0625, ((0, 4), (1, 128)), jnp.float32)
    stream = draw_stream(jax.random.fold_in(arg_keys[5], 71), 0)
    norm_gain = jnp.clip(1.0 + 0.18 * jax.random.normal(arg_keys[3], (D,), jnp.float32), 0.1, 1.9)
    live_rows = draw_live_rows(jax.random.fold_in(arg_keys[5], 71), 0)
    return dict(gate_master=gate_master, up_master=up_master, stream=stream, norm_gain=norm_gain, live_rows=live_rows)


def block_power(largest):
    power_scale = jnp.full(largest.shape, 2.0 ** (-34), largest.dtype)
    for exponent in range(-32, 5):
        power_scale = jnp.where(largest >= 2.0 ** exponent, 2.0 ** (exponent - 2), power_scale)
    return power_scale

def snap_grid(ratio):
    magnitude = jnp.abs(ratio)
    level = jnp.zeros_like(ratio)
    for edge, rise in ((0.25, 0.5), (0.75, 0.5), (1.25, 0.5), (1.75, 0.5), (2.5, 1.0), (3.5, 1.0), (5.0, 2.0)):
        level = level + jnp.where(magnitude >= edge, rise, 0.0)
    return jnp.sign(ratio) * level

def pack_blocks(master):
    row_total, col_total = master.shape
    grouped = master.reshape(row_total, col_total // BLOCK, BLOCK)
    largest = lax.optimization_barrier(jnp.max(jnp.abs(grouped), axis=2))
    power_scale = block_power(largest)
    packed = snap_grid(grouped / power_scale[:, :, None]).astype(jnp.bfloat16)
    return (packed.reshape(row_total, col_total), power_scale.astype(jnp.bfloat16))

def unpack_blocks(packed, block_scale):
    row_total, col_total = packed.shape
    grouped = packed.reshape(row_total, col_total // BLOCK, BLOCK).astype(jnp.float32)
    restored = grouped * block_scale[:, :, None].astype(jnp.float32)
    return restored.astype(jnp.bfloat16).reshape(row_total, col_total)

def reference(gate_master, up_master, stream, norm_gain, live_rows):
    gate_weight = unpack_blocks(*pack_blocks(gate_master))
    up_weight = unpack_blocks(*pack_blocks(up_master))
    square_sum = lax.optimization_barrier(jnp.sum(stream * stream, axis=1))
    inverse = lax.rsqrt(square_sum / D + 1e-06)
    normed = (stream * inverse[:, None] * norm_gain[None, :]).astype(jnp.bfloat16)
    normed_wide = normed.astype(jnp.float32)
    gate_sum = jnp.dot(normed_wide, gate_weight.astype(jnp.float32), precision=lax.Precision.HIGHEST)
    up_sum = jnp.dot(normed_wide, up_weight.astype(jnp.float32), precision=lax.Precision.HIGHEST)
    live_scale = live_rows.astype(jnp.float32)[:, None]
    return (jax.nn.silu(gate_sum) * up_sum * live_scale).astype(jnp.bfloat16)
```

```python
import jax
import jax.numpy as jnp
from jax import lax
from jax.experimental import pallas as pl
from jax.experimental.pallas import tpu as pltpu
from jax.sharding import Mesh, PartitionSpec as P

D = 8192
LIVE = 64
ROWS = 128
FEATS = 256
EXTRA = 16
BLOCK_ROWS = LIVE + EXTRA
CHUNK_ROWS = 2 * LIVE + EXTRA
AXES = ("zh", "zl", "yl", "x", "yh", "c")
BF = jnp.bfloat16
F32 = jnp.float32
VMEM_BYTES = 48 * 1024 * 1024


def split3(value):
    hi = value.astype(BF).astype(F32)
    mid = (value - hi).astype(BF).astype(F32)
    lo = (value - hi - mid).astype(BF).astype(F32)
    return hi, mid, lo


def diagonal(size):
    return lax.broadcasted_iota(jnp.int32, (size, size), 0) == lax.broadcasted_iota(jnp.int32, (size, size), 1)


def slot_table(live):
    rows = lax.broadcasted_iota(jnp.int32, (ROWS, ROWS), 0)
    cols = lax.broadcasted_iota(jnp.int32, (ROWS, ROWS), 1)
    before = jnp.where(rows <= cols, 1.0, 0.0).astype(BF)
    wide = jnp.broadcast_to(live, (16, ROWS))
    rank = jnp.dot(wide.astype(BF), before, preferred_element_type=F32)[0:1, :]
    slot = lax.broadcasted_iota(jnp.int32, (LIVE, ROWS), 0).astype(F32) + 1.0
    return jnp.where((slot == rank) & (live > 0.5), 1.0, 0.0)


def compact_kernel(stream_ref, gain_ref, live_ref, out_ref):
    stream = stream_ref[...]
    live = live_ref[...].astype(F32)
    table = slot_table(live)
    scaled = (stream * gain_ref[...]).astype(BF)
    rows = jnp.dot(table.astype(BF), scaled, preferred_element_type=F32)
    out_ref[0:LIVE, :] = rows.astype(BF)
    square = jnp.sum(stream * stream, axis=1, keepdims=True)
    square_row = jnp.sum(jnp.where(diagonal(ROWS), square, 0.0), axis=0, keepdims=True)
    hi, mid, lo = split3(square_row)
    index = lax.broadcasted_iota(jnp.int32, (EXTRA, ROWS), 0)
    out_ref[LIVE:, 0:ROWS] = jnp.where(index == 0, live, jnp.where(index == 1, mid, 0.0)).astype(BF)
    out_ref[LIVE:, ROWS:] = jnp.where(index == 0, hi, jnp.where(index == 1, lo, 0.0)).astype(BF)


def compact(stream, gain, live):
    return pl.pallas_call(
        compact_kernel,
        out_shape=jax.ShapeDtypeStruct((BLOCK_ROWS, FEATS), BF),
        name="compact",
    )(stream, gain.reshape(1, FEATS), live.reshape(1, ROWS))


def restore(master):
    tile = master.T.reshape(4, 32, 128)
    size = jnp.abs(tile)
    largest = jnp.max(size, axis=1, keepdims=True)
    wide = largest * 8388609.0
    power = jnp.abs(wide - wide * (1.0 - 2.0**-24))
    power = jnp.where(power > largest, power * 0.5, power)
    power = jnp.where(power * 2.0 <= largest, power * 2.0, power)
    scale = jnp.clip(power, 2.0**-32, 2.0**4) * 0.25
    level = jnp.zeros_like(size)
    for edge, value in ((0.25, 0.5), (0.75, 1.0), (1.25, 1.5), (1.75, 2.0), (2.5, 3.0), (3.5, 4.0), (5.0, 6.0)):
        level = jnp.where(size >= scale * edge, scale * value, level)
    return jnp.where(tile < 0.0, -level, level).reshape(128, 128).T.astype(BF)


def pack_kernel(yl_ref, gate_ref, up_ref, same_ref, flip_ref):
    yl = yl_ref[0]
    for out_ref, half in ((same_ref, yl), (flip_ref, 1 - yl)):
        for tile in range(2):
            rows = pl.ds(pl.multiple_of(half * FEATS + tile * 128, 128), 128)
            out_ref[0, tile * 128 : (tile + 1) * 128, 0:128] = restore(gate_ref[rows, :])
            out_ref[0, tile * 128 : (tile + 1) * 128, 128:256] = restore(up_ref[rows, :])


def pack(yl, gate_master, up_master):
    shape = jax.ShapeDtypeStruct((4, FEATS, 256), BF)
    return pl.pallas_call(
        pack_kernel,
        grid=(4,),
        in_specs=[
            pl.BlockSpec(memory_space=pltpu.SMEM),
            pl.BlockSpec((2 * FEATS, 128), lambda i: (i, 0)),
            pl.BlockSpec((2 * FEATS, 128), lambda i: (i, 0)),
        ],
        out_specs=[pl.BlockSpec((1, FEATS, 256), lambda i: (i, 0, 0))] * 2,
        out_shape=[shape, shape],
        compiler_params=pltpu.CompilerParams(vmem_limit_bytes=VMEM_BYTES),
        name="pack",
    )(yl, gate_master, up_master)


def partial_kernel(y_ref, own_ref, other_ref, w00_ref, w01_ref, w10_ref, w11_ref, out_ref):
    yl, yh = y_ref[0], y_ref[1]
    index = lax.broadcasted_iota(jnp.int32, (EXTRA, ROWS), 0)
    left = [jnp.zeros((EXTRA, ROWS), F32) for _ in range(4)]
    right = [jnp.zeros((EXTRA, ROWS), F32) for _ in range(4)]
    for part, a_ref in enumerate((own_ref, other_ref)):
        for pool in range(4):
            square = jnp.zeros((1, ROWS), F32)
            for block in range(4):
                tail = a_ref[pool, block, LIVE:, :].astype(F32)
                square = square + tail[0:1, ROWS:] + tail[1:2, :ROWS] + tail[1:2, ROWS:]
            live = a_ref[pool, 0, LIVE:, :].astype(F32)[0:1, :ROWS]
            hi, mid, lo = split3(square)
            top, low = index == 2 * part, index == 2 * part + 1
            left[pool] = jnp.where(top, live, jnp.where(low, mid, left[pool]))
            right[pool] = jnp.where(top, hi, jnp.where(low, lo, right[pool]))
    for flip_l, flip_h, w_ref in ((0, 0, w00_ref), (0, 1, w01_ref), (1, 0, w10_ref), (1, 1, w11_ref)):
        to_l, to_h = lax.rem(yl + flip_l, 2), lax.rem(yh + flip_h, 2)
        for part, a_ref in enumerate((own_ref, other_ref)):
            total = jnp.zeros((4 * LIVE, 256), F32)
            for block in range(4):
                rows = a_ref[:, block, 0:LIVE, :].reshape(4 * LIVE, FEATS)
                total = total + jnp.dot(rows, w_ref[block], preferred_element_type=F32)
            for pool in range(4):
                out_ref[to_l, pool, to_h, part * LIVE : (part + 1) * LIVE, :] = total[
                    pool * LIVE : (pool + 1) * LIVE, :
                ].astype(BF)
        for pool in range(4):
            out_ref[to_l, pool, to_h, 2 * LIVE :, 0:ROWS] = left[pool].astype(BF)
            out_ref[to_l, pool, to_h, 2 * LIVE :, ROWS:] = right[pool].astype(BF)


def partial(place, own, other, weights):
    return pl.pallas_call(
        partial_kernel,
        in_specs=[pl.BlockSpec(memory_space=pltpu.SMEM)] + [pl.BlockSpec(memory_space=pltpu.VMEM)] * 6,
        out_specs=pl.BlockSpec(memory_space=pltpu.VMEM),
        out_shape=jax.ShapeDtypeStruct((2, 4, 2, CHUNK_ROWS, 256), BF),
        compiler_params=pltpu.CompilerParams(vmem_limit_bytes=VMEM_BYTES),
        name="partial",
    )(place, own, other, *weights)


def finish_kernel(c_ref, in_ref, out_ref):
    c = c_ref[0]
    for yh in range(2):
        total = jnp.zeros((2 * LIVE, 256), F32)
        square = [jnp.zeros((1, ROWS), F32) for _ in range(2)]
        for yl in range(2):
            for pool in range(4):
                total = total + in_ref[yl, pool, yh, 0 : 2 * LIVE, :].astype(F32)
                tail = in_ref[yl, pool, yh, 2 * LIVE :, :].astype(F32)
                for part in range(2):
                    top, low = 2 * part, 2 * part + 1
                    square[part] = (
                        square[part] + tail[top : top + 1, ROWS:] + tail[low : low + 1, :ROWS] + tail[low : low + 1, ROWS:]
                    )
        tail = in_ref[0, 0, yh, 2 * LIVE :, :].astype(F32)
        for part in range(2):
            table = slot_table(tail[2 * part : 2 * part + 1, :ROWS])
            inverse = lax.rsqrt(square[part] * (1.0 / D) + 1e-06)
            inverse = jnp.sum(table * inverse, axis=1, keepdims=True)
            rows = total[part * LIVE : (part + 1) * LIVE, :] * inverse
            gate, up = rows[:, :128], rows[:, 128:]
            hidden = (gate / (1.0 + jnp.exp(-gate)) * up).astype(BF)
            spread = lax.dot_general(table.astype(BF), hidden, (((0,), (0,)), ((), ())), preferred_element_type=F32)
            block = 2 * yh + lax.rem(c + part, 2)
            out_ref[pl.ds(pl.multiple_of(block * ROWS, ROWS), ROWS), :] = spread.astype(BF)


def finish(c, received):
    return pl.pallas_call(
        finish_kernel,
        in_specs=[pl.BlockSpec(memory_space=pltpu.SMEM), pl.BlockSpec(memory_space=pltpu.VMEM)],
        out_specs=pl.BlockSpec(memory_space=pltpu.VMEM),
        out_shape=jax.ShapeDtypeStruct((4 * ROWS, 128), BF),
        compiler_params=pltpu.CompilerParams(vmem_limit_bytes=VMEM_BYTES),
        name="finish",
    )(c, received)


def shards(gate_master, up_master, stream, norm_gain, live_rows):
    yl = lax.axis_index("yl")
    place = jnp.stack([yl, lax.axis_index("yh")]).astype(jnp.int32)
    core = lax.axis_index("c").astype(jnp.int32).reshape(1)
    block = compact(stream, norm_gain, live_rows)
    swap = [(zh * 4 + x, x * 4 + zh) for zh in range(4) for x in range(4)]
    block = lax.ppermute(block, ("zh", "x"), swap)
    same, flip = pack(yl.astype(jnp.int32).reshape(1), gate_master, up_master)
    block, same, flip = lax.optimization_barrier((block, same, flip))
    w01 = lax.ppermute(same, "yh", [(0, 1), (1, 0)])
    w10 = lax.ppermute(flip, "yl", [(0, 1), (1, 0)])
    w11 = lax.ppermute(flip, ("yl", "yh"), [(0, 3), (1, 2), (2, 1), (3, 0)])
    own = lax.all_gather(block, ("zh", "zl"), axis=0, tiled=False).reshape(4, 4, BLOCK_ROWS, FEATS)
    own, w01, w10, w11 = lax.optimization_barrier((own, w01, w10, w11))
    other = lax.ppermute(own, "c", [(0, 1), (1, 0)])
    sums = partial(place, own, other, (same, w01, w10, w11))
    sums = sums.reshape(16, CHUNK_ROWS, 256)
    received = lax.all_to_all(sums, ("yl", "x", "yh"), 0, 0)
    return finish(core, received.reshape(2, 4, 2, CHUNK_ROWS, 256))


def solution(mesh):
    fine = Mesh(mesh.devices.reshape(4, 4, 2, 4, 2, 2), AXES)
    learner, tp = ("zh", "zl", "yl"), ("yh", "c")
    placed = (
        P("x", learner + tp),
        P("x", learner + tp),
        P(("x",) + tp, learner),
        P(learner),
        P(("x",) + tp),
    )
    return jax.shard_map(shards, mesh=fine, in_specs=placed, out_specs=P("x", learner + tp), check_vma=False)
```

```python
import jax
import jax.numpy as jnp
from jax import lax
from jax.experimental import pallas as pl
from jax.experimental.pallas import tpu as pltpu
from jax.sharding import Mesh, PartitionSpec as P

D = 8192
LIVE = 64
ROWS = 128
FEATS = 256
EXTRA = 8
BLOCK_ROWS = LIVE + EXTRA
CHUNK_ROWS = 2 * LIVE + EXTRA
AXES = ("zh", "zl", "yl", "x", "yh", "c")
BF = jnp.bfloat16
F32 = jnp.float32
VMEM_BYTES = 48 * 1024 * 1024


def split3(value):
    hi = value.astype(BF).astype(F32)
    mid = (value - hi).astype(BF).astype(F32)
    lo = (value - hi - mid).astype(BF).astype(F32)
    return hi, mid, lo


def diagonal(size):
    return lax.broadcasted_iota(jnp.int32, (size, size), 0) == lax.broadcasted_iota(jnp.int32, (size, size), 1)


def slot_table(live):
    rows = lax.broadcasted_iota(jnp.int32, (ROWS, ROWS), 0)
    cols = lax.broadcasted_iota(jnp.int32, (ROWS, ROWS), 1)
    before = jnp.where(rows <= cols, 1.0, 0.0).astype(BF)
    wide = jnp.broadcast_to(live, (16, ROWS))
    rank = jnp.dot(wide.astype(BF), before, preferred_element_type=F32)[0:1, :]
    slot = lax.broadcasted_iota(jnp.int32, (LIVE, ROWS), 0).astype(F32) + 1.0
    return jnp.where((slot == rank) & (live > 0.5), 1.0, 0.0)


def compact_kernel(stream_ref, gain_ref, live_ref, out_ref):
    stream = stream_ref[...]
    live = live_ref[...].astype(F32)
    table = slot_table(live)
    scaled = (stream * gain_ref[...]).astype(BF)
    rows = jnp.dot(table.astype(BF), scaled, preferred_element_type=F32)
    out_ref[0:LIVE, :] = rows.astype(BF)
    square = jnp.sum(stream * stream, axis=1, keepdims=True)
    square_row = jnp.sum(jnp.where(diagonal(ROWS), square, 0.0), axis=0, keepdims=True)
    hi, mid, lo = split3(square_row)
    index = lax.broadcasted_iota(jnp.int32, (EXTRA, ROWS), 0)
    out_ref[LIVE:, 0:ROWS] = jnp.where(index == 0, live, jnp.where(index == 1, mid, 0.0)).astype(BF)
    out_ref[LIVE:, ROWS:] = jnp.where(index == 0, hi, jnp.where(index == 1, lo, 0.0)).astype(BF)


def compact(stream, gain, live):
    return pl.pallas_call(
        compact_kernel,
        out_shape=jax.ShapeDtypeStruct((BLOCK_ROWS, FEATS), BF),
        name="compact",
    )(stream, gain.reshape(1, FEATS), live.reshape(1, ROWS))


def restore(master):
    tile = master.T.reshape(4, 32, 128)
    size = jnp.abs(tile)
    largest = jnp.max(size, axis=1, keepdims=True)
    wide = largest * 8388609.0
    power = jnp.abs(wide - wide * (1.0 - 2.0**-24))
    power = jnp.where(power > largest, power * 0.5, power)
    power = jnp.where(power * 2.0 <= largest, power * 2.0, power)
    scale = jnp.clip(power, 2.0**-32, 2.0**4) * 0.25
    level = jnp.zeros_like(size)
    for edge, value in ((0.25, 0.5), (0.75, 1.0), (1.25, 1.5), (1.75, 2.0), (2.5, 3.0), (3.5, 4.0), (5.0, 6.0)):
        level = jnp.where(size >= scale * edge, scale * value, level)
    return jnp.where(tile < 0.0, -level, level).reshape(128, 128).T.astype(BF)


def pack_kernel(gate_ref, up_ref, out_ref):
    for half in range(2):
        for tile in range(2):
            rows = slice(half * FEATS + tile * 128, half * FEATS + (tile + 1) * 128)
            for side, ref in enumerate((gate_ref, up_ref)):
                value = restore(ref[rows, :])
                for copy in range(2):
                    out_ref[2 * half + copy, 0, tile * 128 : (tile + 1) * 128, side * 128 : (side + 1) * 128] = value


def pack(gate_master, up_master):
    return pl.pallas_call(
        pack_kernel,
        grid=(4,),
        in_specs=[pl.BlockSpec((2 * FEATS, 128), lambda i: (i, 0))] * 2,
        out_specs=pl.BlockSpec((4, 1, FEATS, 256), lambda i: (0, i, 0, 0)),
        out_shape=jax.ShapeDtypeStruct((4, 4, FEATS, 256), BF),
        compiler_params=pltpu.CompilerParams(vmem_limit_bytes=VMEM_BYTES),
        name="pack",
    )(gate_master, up_master)


def offset(apart, zl):
    reach = (6, 4, 0, 2)[apart]
    return zl - reach if zl < 2 else zl + reach


def partial_kernel(x_ref, own_ref, other_ref, w_ref, out_ref):
    x = x_ref[0]
    index = lax.broadcasted_iota(jnp.int32, (EXTRA, ROWS), 0)
    places = [[lax.rem(4 * x + 16 + offset(apart, zl), 16) for zl in range(4)] for apart in range(4)]
    pools = [lax.rem(x + apart, 4) for apart in range(4)]
    for apart in range(4):
        left = jnp.zeros((EXTRA, ROWS), F32)
        right = jnp.zeros((EXTRA, ROWS), F32)
        for part, a_ref in enumerate((own_ref, other_ref)):
            square = jnp.zeros((1, ROWS), F32)
            for zl in range(4):
                tail = a_ref[places[apart][zl], LIVE:, :].astype(F32)
                square = square + tail[0:1, ROWS:] + tail[1:2, :ROWS] + tail[1:2, ROWS:]
            live = tail[0:1, :ROWS]
            hi, mid, lo = split3(square)
            top, low = index == 2 * part, index == 2 * part + 1
            left = jnp.where(top, live, jnp.where(low, mid, left))
            right = jnp.where(top, hi, jnp.where(low, lo, right))
        for to_l in range(2):
            for to_h in range(2):
                out_ref[to_l, pools[apart], to_h, 2 * LIVE :, 0:ROWS] = left.astype(BF)
                out_ref[to_l, pools[apart], to_h, 2 * LIVE :, ROWS:] = right.astype(BF)
    for part, a_ref in enumerate((own_ref, other_ref)):
        rows = [
            jnp.concatenate([a_ref[places[apart][zl], 0:LIVE, :] for apart in range(4)], axis=0) for zl in range(4)
        ]
        for to_l in range(2):
            for to_h in range(2):
                total = jnp.zeros((4 * LIVE, 256), F32)
                for zl in range(4):
                    total = total + jnp.dot(rows[zl], w_ref[2 * to_l + to_h, zl], preferred_element_type=F32)
                for apart in range(4):
                    out_ref[to_l, pools[apart], to_h, part * LIVE : (part + 1) * LIVE, :] = total[
                        apart * LIVE : (apart + 1) * LIVE, :
                    ].astype(BF)


def partial(x, own, other, weights):
    return pl.pallas_call(
        partial_kernel,
        in_specs=[pl.BlockSpec(memory_space=pltpu.SMEM)] + [pl.BlockSpec(memory_space=pltpu.VMEM)] * 3,
        out_specs=pl.BlockSpec(memory_space=pltpu.VMEM),
        out_shape=jax.ShapeDtypeStruct((2, 4, 2, CHUNK_ROWS, 256), BF),
        compiler_params=pltpu.CompilerParams(vmem_limit_bytes=VMEM_BYTES),
        name="partial",
    )(x, own, other, weights)


def finish_kernel(c_ref, in_ref, out_ref):
    c = c_ref[0]
    for yh in range(2):
        total = jnp.zeros((2 * LIVE, 256), F32)
        square = [jnp.zeros((1, ROWS), F32) for _ in range(2)]
        for yl in range(2):
            for pool in range(4):
                total = total + in_ref[yl, pool, yh, 0 : 2 * LIVE, :].astype(F32)
                tail = in_ref[yl, pool, yh, 2 * LIVE :, :].astype(F32)
                for part in range(2):
                    top, low = 2 * part, 2 * part + 1
                    square[part] = (
                        square[part] + tail[top : top + 1, ROWS:] + tail[low : low + 1, :ROWS] + tail[low : low + 1, ROWS:]
                    )
        tail = in_ref[0, 0, yh, 2 * LIVE :, :].astype(F32)
        for part in range(2):
            table = slot_table(tail[2 * part : 2 * part + 1, :ROWS])
            inverse = lax.rsqrt(square[part] * (1.0 / D) + 1e-06)
            inverse = jnp.sum(table * inverse, axis=1, keepdims=True)
            rows = total[part * LIVE : (part + 1) * LIVE, :] * inverse
            gate, up = rows[:, :128], rows[:, 128:]
            hidden = (gate / (1.0 + jnp.exp(-gate)) * up).astype(BF)
            spread = lax.dot_general(table.astype(BF), hidden, (((0,), (0,)), ((), ())), preferred_element_type=F32)
            block = 2 * yh + lax.rem(c + part, 2)
            out_ref[pl.ds(pl.multiple_of(block * ROWS, ROWS), ROWS), :] = spread.astype(BF)


def finish(c, received):
    return pl.pallas_call(
        finish_kernel,
        in_specs=[pl.BlockSpec(memory_space=pltpu.SMEM), pl.BlockSpec(memory_space=pltpu.VMEM)],
        out_specs=pl.BlockSpec(memory_space=pltpu.VMEM),
        out_shape=jax.ShapeDtypeStruct((4 * ROWS, 128), BF),
        compiler_params=pltpu.CompilerParams(vmem_limit_bytes=VMEM_BYTES),
        name="finish",
    )(c, received)


def slab_moves():
    moves = []
    for p in range(4):
        for apart in range(4):
            for zl in range(4):
                moves.append(((4 * p + zl) * 4 + (p + apart) % 4, (4 * p + offset(apart, zl)) % 16 * 4 + p))
    return moves


def shards(gate_master, up_master, stream, norm_gain, live_rows):
    core = lax.axis_index("c").astype(jnp.int32).reshape(1)
    x = lax.axis_index("x").astype(jnp.int32).reshape(1)
    block = compact(stream, norm_gain, live_rows)
    block = lax.ppermute(block, ("zh", "zl", "x"), slab_moves())
    weights = pack(gate_master, up_master)
    block, weights = lax.optimization_barrier((block, weights))
    weights = lax.all_to_all(weights, ("yl", "yh"), 0, 0)
    own = lax.all_gather(block, ("zh", "zl"), axis=0, tiled=False)
    own, weights = lax.optimization_barrier((own, weights))
    other = lax.ppermute(own, "c", [(0, 1), (1, 0)])
    sums = partial(x, own, other, weights)
    sums = sums.reshape(16, CHUNK_ROWS, 256)
    received = lax.all_to_all(sums, ("yl", "x", "yh"), 0, 0)
    return finish(core, received.reshape(2, 4, 2, CHUNK_ROWS, 256))


def solution(mesh):
    fine = Mesh(mesh.devices.reshape(4, 4, 2, 4, 2, 2), AXES)
    learner, tp = ("zh", "zl", "yl"), ("yh", "c")
    placed = (
        P("x", learner + tp),
        P("x", learner + tp),
        P(("x",) + tp, learner),
        P(learner),
        P(("x",) + tp),
    )
    return jax.shard_map(shards, mesh=fine, in_specs=placed, out_specs=P("x", learner + tp), check_vma=False)
```

```python
import jax
import jax.numpy as jnp
from jax import lax
from jax.experimental import pallas as pl
from jax.experimental.pallas import tpu as pltpu
from jax.sharding import Mesh, PartitionSpec as P

D = 8192
LIVE = 64
ROWS = 128
FEATS = 256
EXTRA = 8
BLOCK_ROWS = LIVE + EXTRA
AXES = ("zh", "zl", "yl", "x", "yh", "c")
BF = jnp.bfloat16
F32 = jnp.float32
VMEM_BYTES = 24 * 1024 * 1024


def split3(value):
    hi = value.astype(BF).astype(F32)
    mid = (value - hi).astype(BF).astype(F32)
    lo = (value - hi - mid).astype(BF).astype(F32)
    return hi, mid, lo


def diagonal(size):
    return lax.broadcasted_iota(jnp.int32, (size, size), 0) == lax.broadcasted_iota(jnp.int32, (size, size), 1)


def slot_table(live):
    rows = lax.broadcasted_iota(jnp.int32, (ROWS, ROWS), 0)
    cols = lax.broadcasted_iota(jnp.int32, (ROWS, ROWS), 1)
    before = jnp.where(rows <= cols, 1.0, 0.0).astype(BF)
    wide = jnp.broadcast_to(live, (16, ROWS))
    rank = jnp.dot(wide.astype(BF), before, preferred_element_type=F32)[0:1, :]
    slot = lax.broadcasted_iota(jnp.int32, (LIVE, ROWS), 0).astype(F32) + 1.0
    return jnp.where((slot == rank) & (live > 0.5), 1.0, 0.0)


def restore(master):
    tile = master.T.reshape(4, 32, 128)
    size = jnp.abs(tile)
    largest = jnp.max(size, axis=1, keepdims=True)
    wide = largest * 8388609.0
    power = jnp.abs(wide - wide * (1.0 - 2.0**-24))
    power = jnp.where(power > largest, power * 0.5, power)
    power = jnp.where(power * 2.0 <= largest, power * 2.0, power)
    scale = jnp.clip(power, 2.0**-32, 2.0**4) * 0.25
    level = jnp.zeros_like(size)
    for edge, value in ((0.25, 0.5), (0.75, 1.0), (1.25, 1.5), (1.75, 2.0), (2.5, 3.0), (3.5, 4.0), (5.0, 6.0)):
        level = jnp.where(size >= scale * edge, scale * value, level)
    return jnp.where(tile < 0.0, -level, level).reshape(128, 128).T.astype(BF)


def compact(stream, gain, live, block_ref):
    table = slot_table(live)
    scaled = (stream * gain).astype(BF)
    rows = jnp.dot(table.astype(BF), scaled, preferred_element_type=F32)
    block_ref[0:LIVE, :] = rows.astype(BF)
    square = jnp.sum(stream * stream, axis=1, keepdims=True)
    square_row = jnp.sum(jnp.where(diagonal(ROWS), square, 0.0), axis=0, keepdims=True)
    hi, mid, lo = split3(square_row)
    index = lax.broadcasted_iota(jnp.int32, (EXTRA, ROWS), 0)
    block_ref[LIVE:, 0:ROWS] = jnp.where(index == 0, live, jnp.where(index == 1, mid, 0.0)).astype(BF)
    block_ref[LIVE:, ROWS:] = jnp.where(index == 0, hi, jnp.where(index == 1, lo, 0.0)).astype(BF)


def prepare_kernel(
    gate_hbm, up_hbm, stream_hbm, gain_hbm, live_hbm, out_hbm, block_ref,
    gate_ref, up_ref, stream_ref, gain_ref, live_ref, packed_ref, row_sems, in_sems, out_sems,
):
    loads = []
    for zl in range(4):
        rows = pl.ds(zl * 2 * FEATS, 2 * FEATS)
        for side, (hbm, ref) in enumerate(((gate_hbm, gate_ref), (up_hbm, up_ref))):
            load = pltpu.make_async_copy(hbm.at[rows, :], ref.at[rows, :], in_sems.at[zl, side])
            load.start()
            loads.append(load)
    row_loads = []
    for i, (hbm, ref) in enumerate(((stream_hbm, stream_ref), (gain_hbm, gain_ref), (live_hbm, live_ref))):
        load = pltpu.make_async_copy(hbm, ref, row_sems.at[i])
        load.start()
        row_loads.append(load)
    stores = []
    for zl in range(4):
        for side, ref in enumerate((gate_ref, up_ref)):
            loads[2 * zl + side].wait()
            for tile in range(4):
                yl, top = tile // 2, (tile % 2) * 128
                value = restore(ref[zl * 2 * FEATS + tile * 128 : zl * 2 * FEATS + (tile + 1) * 128, :])
                packed_ref[yl, zl, top : top + 128, side * 128 : (side + 1) * 128] = value
        for yl in range(2):
            for x in range(4):
                store = pltpu.make_async_copy(packed_ref.at[yl, zl], out_hbm.at[4 * yl + x, zl], out_sems.at[zl, yl, x])
                store.start()
                stores.append(store)
    for load in row_loads:
        load.wait()
    compact(stream_ref[...], gain_ref[...], live_ref[...].astype(F32), block_ref)
    for store in stores:
        store.wait()


def prepare(gate_master, up_master, stream, gain, live):
    return pl.pallas_call(
        prepare_kernel,
        in_specs=[pl.BlockSpec(memory_space=pl.ANY)] * 5,
        out_specs=[pl.BlockSpec(memory_space=pl.ANY), pl.BlockSpec(memory_space=pltpu.VMEM)],
        out_shape=[jax.ShapeDtypeStruct((8, 4, FEATS, 256), BF), jax.ShapeDtypeStruct((BLOCK_ROWS, FEATS), BF)],
        scratch_shapes=[
            pltpu.VMEM((8 * FEATS, 128), F32),
            pltpu.VMEM((8 * FEATS, 128), F32),
            pltpu.VMEM((ROWS, FEATS), F32),
            pltpu.VMEM((1, FEATS), F32),
            pltpu.VMEM((1, ROWS), jnp.int32),
            pltpu.VMEM((2, 4, FEATS, 256), BF),
            pltpu.SemaphoreType.DMA((3,)),
            pltpu.SemaphoreType.DMA((4, 2)),
            pltpu.SemaphoreType.DMA((4, 2, 4)),
        ],
        compiler_params=pltpu.CompilerParams(vmem_limit_bytes=62 * 1024 * 1024),
        name="prepare",
    )(gate_master, up_master, stream, gain.reshape(1, FEATS), live.reshape(1, ROWS))


def add_up(a_refs, own_ref, sent_ref, square_ref, table_ref, weight):
    index = lax.broadcasted_iota(jnp.int32, (EXTRA, ROWS), 0)
    for i, a_ref in enumerate(a_refs):
        tails = jnp.sum(a_ref[:, LIVE:, :].astype(F32), axis=0)
        square = tails[0:1, ROWS:] + tails[1:2, :ROWS] + tails[1:2, ROWS:]
        hi, mid, lo = split3(square)
        sent_ref[i, LIVE:, 0:ROWS] = jnp.where(index == 1, mid, 0.0).astype(BF)
        sent_ref[i, LIVE:, ROWS:] = jnp.where(index == 0, hi, jnp.where(index == 1, lo, 0.0)).astype(BF)
        square_ref[i] = jnp.broadcast_to(square, (EXTRA, ROWS))
        table_ref[i] = slot_table(a_ref[0, LIVE:, :].astype(F32)[0:1, :ROWS]).astype(BF)
    totals = [jnp.zeros((2 * LIVE, 256), F32) for _ in range(2)]
    for z in range(16):
        rows = jnp.concatenate([a_ref[z, 0:LIVE, :] for a_ref in a_refs], axis=0)
        for other in range(2):
            totals[other] = totals[other] + jnp.dot(rows, weight(other, z), preferred_element_type=F32)
    for i in range(2):
        own_ref[i] = totals[0][i * LIVE : (i + 1) * LIVE, :]
        sent_ref[i, 0:LIVE, :] = totals[1][i * LIVE : (i + 1) * LIVE, :].astype(BF)


def near_kernel(yl_ref, own_a_ref, other_a_ref, w_hbm, own_ref, sent_ref, square_ref, table_ref, w_ref, sems):
    yl = yl_ref[0]
    loads = []
    for x in range(4):
        for other in range(2):
            load = pltpu.make_async_copy(w_hbm.at[4 * (yl ^ other) + x], w_ref.at[4 * other + x], sems.at[x, other])
            load.start()
            loads.append(load)

    def weight(other, z):
        if z % 4 == 0:
            loads[2 * (z // 4) + other].wait()
        return w_ref[4 * other + z // 4, z % 4]

    add_up((own_a_ref, other_a_ref), own_ref, sent_ref, square_ref, table_ref, weight)


def far_kernel(place_ref, own_a_ref, other_a_ref, near_ref, w_ref, own_ref, sent_ref, square_ref, table_ref, far_ref):
    yh, c = place_ref[0], place_ref[1]
    add_up(
        (own_a_ref, other_a_ref), own_ref, far_ref, square_ref, table_ref, lambda other, z: w_ref[4 * other + z // 4, z % 4]
    )
    for flip_h, ref in enumerate((near_ref, far_ref)):
        for flip_c in range(2):
            sent_ref[yh ^ flip_h, c ^ flip_c] = ref[flip_c]


SUM_SHAPES = [
    jax.ShapeDtypeStruct((2, LIVE, 256), F32),
    jax.ShapeDtypeStruct((2, BLOCK_ROWS, 256), BF),
    jax.ShapeDtypeStruct((2, EXTRA, ROWS), F32),
    jax.ShapeDtypeStruct((2, LIVE, ROWS), BF),
]


def near(yl, own_a, other_a, weights):
    vmem = pl.BlockSpec(memory_space=pltpu.VMEM)
    return pl.pallas_call(
        near_kernel,
        in_specs=[pl.BlockSpec(memory_space=pltpu.SMEM), vmem, vmem, pl.BlockSpec(memory_space=pl.ANY)],
        out_specs=[vmem] * 5,
        out_shape=SUM_SHAPES + [jax.ShapeDtypeStruct(weights.shape, BF)],
        scratch_shapes=[pltpu.SemaphoreType.DMA((4, 2))],
        compiler_params=pltpu.CompilerParams(vmem_limit_bytes=VMEM_BYTES),
        name="near",
    )(yl, own_a, other_a, weights)


def far(place, own_a, other_a, near_sent, weights):
    vmem = pl.BlockSpec(memory_space=pltpu.VMEM)
    return pl.pallas_call(
        far_kernel,
        in_specs=[pl.BlockSpec(memory_space=pltpu.SMEM)] + [vmem] * 4,
        out_specs=[vmem] * 4,
        out_shape=[SUM_SHAPES[0], jax.ShapeDtypeStruct((2, 2, BLOCK_ROWS, 256), BF), SUM_SHAPES[2], SUM_SHAPES[3]],
        scratch_shapes=[pltpu.VMEM((2, BLOCK_ROWS, 256), BF)],
        compiler_params=pltpu.CompilerParams(vmem_limit_bytes=VMEM_BYTES),
        name="far",
    )(place, own_a, other_a, near_sent, weights)


def finish_kernel(place_ref, *refs):
    yh, c = place_ref[0], place_ref[1]
    other_ref, out_ref = refs[6], refs[7]
    for flip_h in range(2):
        own_ref, square_ref, table_ref = refs[3 * flip_h : 3 * flip_h + 3]
        for flip_c in range(2):
            sent = other_ref[yh ^ flip_h, c ^ flip_c].astype(F32)
            rows = own_ref[flip_c] + sent[0:LIVE, :]
            tail = sent[LIVE:, :]
            square = square_ref[flip_c, 0:1, :] + tail[0:1, ROWS:] + tail[1:2, :ROWS] + tail[1:2, ROWS:]
            table = table_ref[flip_c]
            inverse = lax.rsqrt(square * (1.0 / D) + 1e-06)
            rows = rows * jnp.sum(table.astype(F32) * inverse, axis=1, keepdims=True)
            gate, up = rows[:, :128], rows[:, 128:]
            hidden = (gate / (1.0 + jnp.exp(-gate)) * up).astype(BF)
            spread = lax.dot_general(table, hidden, (((0,), (0,)), ((), ())), preferred_element_type=F32)
            block = 2 * (yh ^ flip_h) + (c ^ flip_c)
            out_ref[pl.ds(pl.multiple_of(block * ROWS, ROWS), ROWS), :] = spread.astype(BF)


def finish(place, near_sums, far_sums, other):
    return pl.pallas_call(
        finish_kernel,
        in_specs=[pl.BlockSpec(memory_space=pltpu.SMEM)] + [pl.BlockSpec(memory_space=pltpu.VMEM)] * 7,
        out_specs=pl.BlockSpec(memory_space=pltpu.VMEM),
        out_shape=jax.ShapeDtypeStruct((4 * ROWS, 128), BF),
        compiler_params=pltpu.CompilerParams(vmem_limit_bytes=VMEM_BYTES),
        name="finish",
    )(place, *near_sums, *far_sums, other)


def partner_groups():
    return [
        [((yl * 4 + x) * 2 + (h ^ (yl & c))) * 2 + c for yl in range(2) for x in range(4)]
        for h in range(2)
        for c in range(2)
    ]


def partner_moves():
    moves = []
    for yl in range(2):
        for yh in range(2):
            for c in range(2):
                moves.append(((yl * 2 + yh) * 2 + c, ((1 - yl) * 2 + (yh ^ c)) * 2 + c))
    return moves


def shards(gate_master, up_master, stream, norm_gain, live_rows):
    yl = lax.axis_index("yl").astype(jnp.int32).reshape(1)
    place = jnp.stack([lax.axis_index("yh"), lax.axis_index("c")]).astype(jnp.int32)
    weights, block = prepare(gate_master, up_master, stream, norm_gain, live_rows)
    weights = lax.all_to_all(weights, ("yl", "x", "yh", "c"), 0, 0, axis_index_groups=partner_groups())
    a00 = lax.all_gather(block, ("zh", "zl"), axis=0, tiled=False)
    a10 = lax.ppermute(a00, "yh", [(0, 1), (1, 0)])
    a01 = lax.ppermute(a00, "c", [(0, 1), (1, 0)])
    a11 = lax.ppermute(a10, "c", [(0, 1), (1, 0)])
    near_own, near_sent, near_square, near_table, weights = near(yl, a00, a01, weights)
    far_own, sent, far_square, far_table = far(place, a10, a11, near_sent, weights)
    other = lax.ppermute(sent, ("yl", "yh", "c"), partner_moves())
    return finish(place, (near_own, near_square, near_table), (far_own, far_square, far_table), other)


def solution(mesh):
    fine = Mesh(mesh.devices.reshape(4, 4, 2, 4, 2, 2), AXES)
    learner, tp = ("zh", "zl", "yl"), ("yh", "c")
    placed = (
        P("x", learner + tp),
        P("x", learner + tp),
        P(("x",) + tp, learner),
        P(learner),
        P(("x",) + tp),
    )
    return jax.shard_map(shards, mesh=fine, in_specs=placed, out_specs=P("x", learner + tp), check_vma=False)
```

```python
import jax
import jax.numpy as jnp
from jax import lax
from jax.experimental import pallas as pl
from jax.experimental.pallas import tpu as pltpu
from jax.sharding import Mesh, PartitionSpec as P

D = 8192
LIVE = 64
ROWS = 128
FEATS = 256
EXTRA = 8
BLOCK_ROWS = LIVE + EXTRA
EARLY = 48
LATE = LIVE - EARLY
NEAR = LIVE + EARLY
AXES = ("zh", "zl", "yl", "x", "yh", "c")
BF = jnp.bfloat16
F32 = jnp.float32
VMEM_BYTES = 24 * 1024 * 1024


def split3(value):
    hi = value.astype(BF).astype(F32)
    mid = (value - hi).astype(BF).astype(F32)
    lo = (value - hi - mid).astype(BF).astype(F32)
    return hi, mid, lo


def diagonal(size):
    return lax.broadcasted_iota(jnp.int32, (size, size), 0) == lax.broadcasted_iota(jnp.int32, (size, size), 1)


def slot_table(live):
    rows = lax.broadcasted_iota(jnp.int32, (ROWS, ROWS), 0)
    cols = lax.broadcasted_iota(jnp.int32, (ROWS, ROWS), 1)
    before = jnp.where(rows <= cols, 1.0, 0.0).astype(BF)
    wide = jnp.broadcast_to(live, (16, ROWS))
    rank = jnp.dot(wide.astype(BF), before, preferred_element_type=F32)[0:1, :]
    slot = lax.broadcasted_iota(jnp.int32, (LIVE, ROWS), 0).astype(F32) + 1.0
    return jnp.where((slot == rank) & (live > 0.5), 1.0, 0.0)


def compact_kernel(stream_ref, gain_ref, live_ref, block_ref, early_ref):
    stream = stream_ref[...]
    live = live_ref[...].astype(F32)
    table = slot_table(live)
    scaled = (stream * gain_ref[...]).astype(BF)
    rows = jnp.dot(table.astype(BF), scaled, preferred_element_type=F32).astype(BF)
    block_ref[0:LIVE, :] = rows
    early_ref[0:EARLY, :] = rows[0:EARLY, :]
    square = jnp.sum(stream * stream, axis=1, keepdims=True)
    square_row = jnp.sum(jnp.where(diagonal(ROWS), square, 0.0), axis=0, keepdims=True)
    hi, mid, lo = split3(square_row)
    index = lax.broadcasted_iota(jnp.int32, (EXTRA, ROWS), 0)
    for ref, start, first in ((block_ref, LIVE, 0), (early_ref, EARLY, 2)):
        ref[start:, 0:ROWS] = jnp.where(index == first, live, jnp.where(index == first + 1, mid, 0.0)).astype(BF)
        ref[start:, ROWS:] = jnp.where(index == first, hi, jnp.where(index == first + 1, lo, 0.0)).astype(BF)


def compact(stream, gain, live):
    return pl.pallas_call(
        compact_kernel,
        out_shape=[
            jax.ShapeDtypeStruct((BLOCK_ROWS, FEATS), BF),
            jax.ShapeDtypeStruct((EARLY + EXTRA, FEATS), BF),
        ],
        name="compact",
    )(stream, gain.reshape(1, FEATS), live.reshape(1, ROWS))


def join(block, early):
    return jnp.concatenate([block[:LIVE], early[:EARLY], block[LIVE:] + early[EARLY:]], axis=0)


def restore(master):
    tile = master.T.reshape(4, 32, 128)
    size = jnp.abs(tile)
    largest = jnp.max(size, axis=1, keepdims=True)
    wide = largest * 8388609.0
    power = jnp.abs(wide - wide * (1.0 - 2.0**-24))
    power = jnp.where(power > largest, power * 0.5, power)
    power = jnp.where(power * 2.0 <= largest, power * 2.0, power)
    scale = jnp.clip(power, 2.0**-32, 2.0**4) * 0.25
    level = jnp.zeros_like(size)
    for edge, value in ((0.25, 0.5), (0.75, 1.0), (1.25, 1.5), (1.75, 2.0), (2.5, 3.0), (3.5, 4.0), (5.0, 6.0)):
        level = jnp.where(size >= scale * edge, scale * value, level)
    return jnp.where(tile < 0.0, -level, level).reshape(128, 128).T.astype(BF)


def pack_kernel(gate_hbm, up_hbm, out_hbm, gate_ref, up_ref, packed_ref, in_sems, out_sems):
    loads = []
    for zl in range(4):
        rows = pl.ds(zl * 2 * FEATS, 2 * FEATS)
        for side, (hbm, ref) in enumerate(((gate_hbm, gate_ref), (up_hbm, up_ref))):
            load = pltpu.make_async_copy(hbm.at[rows, :], ref.at[rows, :], in_sems.at[zl, side])
            load.start()
            loads.append(load)
    stores = []
    for zl in range(4):
        loads[2 * zl].wait()
        loads[2 * zl + 1].wait()
        for yl in range(2):
            for side, ref in enumerate((gate_ref, up_ref)):
                for tile in range(2):
                    first = (2 * zl + yl) * FEATS + tile * 128
                    value = restore(ref[first : first + 128, :])
                    packed_ref[yl, zl, tile * 128 : (tile + 1) * 128, side * 128 : (side + 1) * 128] = value
            for x in range(4):
                store = pltpu.make_async_copy(packed_ref.at[yl, zl], out_hbm.at[4 * yl + x, zl], out_sems.at[zl, yl, x])
                store.start()
                stores.append(store)
    for store in stores:
        store.wait()


def pack(gate_master, up_master):
    return pl.pallas_call(
        pack_kernel,
        in_specs=[pl.BlockSpec(memory_space=pl.ANY)] * 2,
        out_specs=pl.BlockSpec(memory_space=pl.ANY),
        out_shape=jax.ShapeDtypeStruct((8, 4, FEATS, 256), BF),
        scratch_shapes=[
            pltpu.VMEM((8 * FEATS, 128), F32),
            pltpu.VMEM((8 * FEATS, 128), F32),
            pltpu.VMEM((2, 4, FEATS, 256), BF),
            pltpu.SemaphoreType.DMA((4, 2)),
            pltpu.SemaphoreType.DMA((4, 2, 4)),
        ],
        compiler_params=pltpu.CompilerParams(vmem_limit_bytes=62 * 1024 * 1024),
        name="pack",
    )(gate_master, up_master)


def square_rows(a_ref):
    tails = jnp.sum(a_ref[:, NEAR:, :].astype(F32), axis=0)
    return [tails[t : t + 1, ROWS:] + tails[t + 1 : t + 2, :ROWS] + tails[t + 1 : t + 2, ROWS:] for t in (0, 2)]


def fetch(w_hbm, w_ref, sems, first):
    loads = [pltpu.make_async_copy(w_hbm.at[first + x], w_ref.at[x], sems.at[x]) for x in range(4)]
    for load in loads:
        load.start()
    return loads


def multiply(rows_refs, w_ref, loads):
    own_a_ref, other_a_ref, own_late_ref, other_late_ref = rows_refs
    pieces = ((own_a_ref, NEAR), (own_late_ref, LATE), (other_a_ref, NEAR), (other_late_ref, LATE))
    total = jnp.zeros((4 * LIVE, 256), F32)
    for load in loads:
        load.wait()
    for z in range(16):
        rows = jnp.concatenate([ref[z, 0:count, :] for ref, count in pieces], axis=0)
        total = total + jnp.dot(rows, w_ref[z // 4, z % 4], preferred_element_type=F32)
    return total


def sent_kernel(place_ref, own_a_ref, other_a_ref, own_late_ref, other_late_ref, w_hbm, sent_ref, w_ref, sems):
    yl, yh, c = place_ref[0], place_ref[1], place_ref[2]
    loads = fetch(w_hbm, w_ref, sems, 4 * (1 - yl))
    index = lax.broadcasted_iota(jnp.int32, (EXTRA, ROWS), 0)
    for i, a_ref in enumerate((own_a_ref, other_a_ref)):
        for flip_h, square in enumerate(square_rows(a_ref)):
            hi, mid, lo = split3(square)
            left = jnp.where(index == 1, mid, 0.0)
            right = jnp.where(index == 0, hi, jnp.where(index == 1, lo, 0.0))
            sent_ref[yh ^ flip_h, c ^ i, LIVE:, 0:ROWS] = left.astype(BF)
            sent_ref[yh ^ flip_h, c ^ i, LIVE:, ROWS:] = right.astype(BF)
    total = multiply((own_a_ref, other_a_ref, own_late_ref, other_late_ref), w_ref, loads)
    for i in range(2):
        for flip_h in range(2):
            first = (2 * i + flip_h) * LIVE
            sent_ref[yh ^ flip_h, c ^ i, 0:LIVE, :] = total[first : first + LIVE, :].astype(BF)


def own_kernel(
    place_ref, own_a_ref, other_a_ref, own_late_ref, other_late_ref, w_hbm,
    own_ref, square_ref, table_ref, w_ref, sems,
):
    loads = fetch(w_hbm, w_ref, sems, 4 * place_ref[0])
    total = multiply((own_a_ref, other_a_ref, own_late_ref, other_late_ref), w_ref, loads)
    for i, a_ref in enumerate((own_a_ref, other_a_ref)):
        lives = a_ref[0, NEAR:, :].astype(F32)
        for flip_h, square in enumerate(square_rows(a_ref)):
            square_ref[i, flip_h] = jnp.broadcast_to(square, (EXTRA, ROWS))
            table_ref[i, flip_h] = slot_table(lives[2 * flip_h : 2 * flip_h + 1, :ROWS]).astype(BF)
            first = (2 * i + flip_h) * LIVE
            own_ref[i, flip_h] = total[first : first + LIVE, :]


def partial(kernel, name, place, rows, weights, out_shape):
    vmem = pl.BlockSpec(memory_space=pltpu.VMEM)
    return pl.pallas_call(
        kernel,
        in_specs=[pl.BlockSpec(memory_space=pltpu.SMEM)] + [vmem] * 4 + [pl.BlockSpec(memory_space=pl.ANY)],
        out_specs=[vmem] * len(out_shape),
        out_shape=out_shape,
        scratch_shapes=[pltpu.VMEM((4, 4, FEATS, 256), BF), pltpu.SemaphoreType.DMA((4,))],
        compiler_params=pltpu.CompilerParams(vmem_limit_bytes=VMEM_BYTES),
        name=name,
    )(place, *rows, weights)


SENT_SHAPES = [jax.ShapeDtypeStruct((2, 2, BLOCK_ROWS, 256), BF)]
OWN_SHAPES = [
    jax.ShapeDtypeStruct((2, 2, LIVE, 256), F32),
    jax.ShapeDtypeStruct((2, 2, EXTRA, ROWS), F32),
    jax.ShapeDtypeStruct((2, 2, LIVE, ROWS), BF),
]


def finish_kernel(place_ref, own_ref, square_ref, table_ref, other_ref, out_ref):
    yh, c = place_ref[1], place_ref[2]
    for flip_h in range(2):
        for i in range(2):
            sent = other_ref[yh ^ flip_h, c ^ i].astype(F32)
            rows = own_ref[i, flip_h] + sent[0:LIVE, :]
            tail = sent[LIVE:, :]
            square = square_ref[i, flip_h, 0:1, :] + tail[0:1, ROWS:] + tail[1:2, :ROWS] + tail[1:2, ROWS:]
            table = table_ref[i, flip_h]
            inverse = lax.rsqrt(square * (1.0 / D) + 1e-06)
            rows = rows * jnp.sum(table.astype(F32) * inverse, axis=1, keepdims=True)
            gate, up = rows[:, :128], rows[:, 128:]
            hidden = (gate / (1.0 + jnp.exp(-gate)) * up).astype(BF)
            spread = lax.dot_general(table, hidden, (((0,), (0,)), ((), ())), preferred_element_type=F32)
            block = 2 * (yh ^ flip_h) + (c ^ i)
            out_ref[pl.ds(pl.multiple_of(block * ROWS, ROWS), ROWS), :] = spread.astype(BF)


def finish(place, own, square, table, other):
    return pl.pallas_call(
        finish_kernel,
        in_specs=[pl.BlockSpec(memory_space=pltpu.SMEM)] + [pl.BlockSpec(memory_space=pltpu.VMEM)] * 4,
        out_specs=pl.BlockSpec(memory_space=pltpu.VMEM),
        out_shape=jax.ShapeDtypeStruct((4 * ROWS, 128), BF),
        compiler_params=pltpu.CompilerParams(vmem_limit_bytes=VMEM_BYTES),
        name="finish",
    )(place, own, square, table, other)


def partner_groups():
    return [
        [((yl * 4 + x) * 2 + (h ^ (yl & c))) * 2 + c for yl in range(2) for x in range(4)]
        for h in range(2)
        for c in range(2)
    ]


def partner_moves():
    moves = []
    for yl in range(2):
        for yh in range(2):
            for c in range(2):
                moves.append(((yl * 2 + yh) * 2 + c, ((1 - yl) * 2 + (yh ^ c)) * 2 + c))
    return moves


def shards(gate_master, up_master, stream, norm_gain, live_rows):
    swap = [(0, 1), (1, 0)]
    place = jnp.stack([lax.axis_index(name) for name in ("yl", "yh", "c")]).astype(jnp.int32)
    block, early = compact(stream, norm_gain, live_rows)
    early = lax.ppermute(early, "yh", swap)
    gate_master, block = lax.optimization_barrier((gate_master, block))
    weights = pack(gate_master, up_master)
    early, weights = lax.optimization_barrier((early, weights))
    weights = lax.all_to_all(weights, ("yl", "x", "yh", "c"), 0, 0, axis_index_groups=partner_groups())
    own_a = lax.all_gather(join(block, early), ("zh", "zl"), axis=0, tiled=False)
    own_late = lax.ppermute(own_a[:, EARLY:LIVE, :], "yh", swap)
    own_a, own_late = lax.optimization_barrier((own_a, own_late))
    other_a = lax.ppermute(own_a, "c", swap)
    other_late = lax.ppermute(own_late, "c", swap)
    rows = (own_a, other_a, own_late, other_late)
    (sent,) = partial(sent_kernel, "sent_sums", place, rows, weights, SENT_SHAPES)
    other = lax.ppermute(sent, ("yl", "yh", "c"), partner_moves())
    own, square, table = partial(own_kernel, "own_sums", place, rows, weights, OWN_SHAPES)
    return finish(place, own, square, table, other)


def solution(mesh):
    fine = Mesh(mesh.devices.reshape(4, 4, 2, 4, 2, 2), AXES)
    learner, tp = ("zh", "zl", "yl"), ("yh", "c")
    placed = (
        P("x", learner + tp),
        P("x", learner + tp),
        P(("x",) + tp, learner),
        P(learner),
        P(("x",) + tp),
    )
    return jax.shard_map(shards, mesh=fine, in_specs=placed, out_specs=P("x", learner + tp), check_vma=False)
```

```python
import jax
import jax.numpy as jnp
from jax import lax
from jax.experimental import pallas as pl
from jax.experimental.pallas import tpu as pltpu
from jax.sharding import Mesh, PartitionSpec as P

D = 8192
LIVE = 64
ROWS = 128
FEATS = 256
EXTRA = 8
BLOCK_ROWS = LIVE + EXTRA
EARLY = 48
LATE = LIVE - EARLY
NEAR = LIVE + EARLY
AXES = ("zh", "zl", "yl", "x", "yh", "c")
BF = jnp.bfloat16
F32 = jnp.float32
VMEM_BYTES = 24 * 1024 * 1024


def split3(value):
    hi = value.astype(BF).astype(F32)
    mid = (value - hi).astype(BF).astype(F32)
    lo = (value - hi - mid).astype(BF).astype(F32)
    return hi, mid, lo


def diagonal(size):
    return lax.broadcasted_iota(jnp.int32, (size, size), 0) == lax.broadcasted_iota(jnp.int32, (size, size), 1)


def slot_table(live):
    rows = lax.broadcasted_iota(jnp.int32, (ROWS, ROWS), 0)
    cols = lax.broadcasted_iota(jnp.int32, (ROWS, ROWS), 1)
    before = jnp.where(rows <= cols, 1.0, 0.0).astype(BF)
    wide = jnp.broadcast_to(live, (16, ROWS))
    rank = jnp.dot(wide.astype(BF), before, preferred_element_type=F32)[0:1, :]
    slot = lax.broadcasted_iota(jnp.int32, (LIVE, ROWS), 0).astype(F32) + 1.0
    return jnp.where((slot == rank) & (live > 0.5), 1.0, 0.0)


def compact_kernel(stream_ref, gain_ref, live_ref, block_ref, early_ref):
    stream = stream_ref[...]
    live = live_ref[...].astype(F32)
    table = slot_table(live)
    scaled = (stream * gain_ref[...]).astype(BF)
    rows = jnp.dot(table.astype(BF), scaled, preferred_element_type=F32).astype(BF)
    block_ref[0:LIVE, :] = rows
    early_ref[0:EARLY, :] = rows[0:EARLY, :]
    square = jnp.sum(stream * stream, axis=1, keepdims=True)
    square_row = jnp.sum(jnp.where(diagonal(ROWS), square, 0.0), axis=0, keepdims=True)
    hi, mid, lo = split3(square_row)
    index = lax.broadcasted_iota(jnp.int32, (EXTRA, ROWS), 0)
    for ref, start, first in ((block_ref, LIVE, 0), (early_ref, EARLY, 2)):
        ref[start:, 0:ROWS] = jnp.where(index == first, live, jnp.where(index == first + 1, mid, 0.0)).astype(BF)
        ref[start:, ROWS:] = jnp.where(index == first, hi, jnp.where(index == first + 1, lo, 0.0)).astype(BF)


def compact(stream, gain, live):
    return pl.pallas_call(
        compact_kernel,
        out_shape=[
            jax.ShapeDtypeStruct((BLOCK_ROWS, FEATS), BF),
            jax.ShapeDtypeStruct((EARLY + EXTRA, FEATS), BF),
        ],
        name="compact",
    )(stream, gain.reshape(1, FEATS), live.reshape(1, ROWS))


def join(block, early):
    return jnp.concatenate([block[:LIVE], early[:EARLY], block[LIVE:] + early[EARLY:]], axis=0)


def power_below(value):
    wide = value * 8388609.0
    return jnp.abs(wide - wide * (1.0 - 2.0**-24))


def restore(master):
    tile = master.T.reshape(4, 32, 128)
    size = jnp.abs(tile)
    largest = jnp.max(size, axis=1, keepdims=True)
    power = power_below(largest)
    power = jnp.where(power > largest, power * 0.5, power)
    power = jnp.where(power * 2.0 <= largest, power * 2.0, power)
    scale = jnp.clip(power, 2.0**-32, 2.0**4) * 0.25
    inverse = power_below((4.0 / scale) * (1.0 + 2.0**-10))
    quarters = jnp.floor(size * inverse)
    step = jnp.where(quarters < 8.0, 1.5 * 2.0**24, jnp.where(quarters < 16.0, 1.5 * 2.0**25, 1.5 * 2.0**26))
    level = jnp.minimum((quarters + 0.5 + step) - step, 24.0)
    quarter = scale * 0.25
    return (level * jnp.where(tile < 0.0, -quarter, quarter)).reshape(128, 128).T.astype(BF)


def pack_kernel(gate_hbm, up_hbm, out_hbm, gate_ref, up_ref, packed_ref, in_sems, out_sems):
    loads = []
    for zl in range(4):
        rows = pl.ds(zl * 2 * FEATS, 2 * FEATS)
        for side, (hbm, ref) in enumerate(((gate_hbm, gate_ref), (up_hbm, up_ref))):
            load = pltpu.make_async_copy(hbm.at[rows, :], ref.at[rows, :], in_sems.at[zl, side])
            load.start()
            loads.append(load)
    stores = []
    for zl in range(4):
        loads[2 * zl].wait()
        loads[2 * zl + 1].wait()
        for yl in range(2):
            for side, ref in enumerate((gate_ref, up_ref)):
                for tile in range(2):
                    first = (2 * zl + yl) * FEATS + tile * 128
                    value = restore(ref[first : first + 128, :])
                    packed_ref[yl, zl, tile * 128 : (tile + 1) * 128, side * 128 : (side + 1) * 128] = value
            for x in range(4):
                store = pltpu.make_async_copy(packed_ref.at[yl, zl], out_hbm.at[4 * yl + x, zl], out_sems.at[zl, yl, x])
                store.start()
                stores.append(store)
    for store in stores:
        store.wait()


def pack(gate_master, up_master):
    return pl.pallas_call(
        pack_kernel,
        in_specs=[pl.BlockSpec(memory_space=pl.ANY)] * 2,
        out_specs=pl.BlockSpec(memory_space=pl.ANY),
        out_shape=jax.ShapeDtypeStruct((8, 4, FEATS, 256), BF),
        scratch_shapes=[
            pltpu.VMEM((8 * FEATS, 128), F32),
            pltpu.VMEM((8 * FEATS, 128), F32),
            pltpu.VMEM((2, 4, FEATS, 256), BF),
            pltpu.SemaphoreType.DMA((4, 2)),
            pltpu.SemaphoreType.DMA((4, 2, 4)),
        ],
        compiler_params=pltpu.CompilerParams(vmem_limit_bytes=62 * 1024 * 1024),
        name="pack",
    )(gate_master, up_master)


def square_rows(a_ref):
    tails = jnp.sum(a_ref[:, NEAR:, :].astype(F32), axis=0)
    return [tails[t : t + 1, ROWS:] + tails[t + 1 : t + 2, :ROWS] + tails[t + 1 : t + 2, ROWS:] for t in (0, 2)]


def fetch(w_hbm, w_ref, sems, first):
    loads = [pltpu.make_async_copy(w_hbm.at[first + x], w_ref.at[x], sems.at[x]) for x in range(4)]
    for load in loads:
        load.start()
    return loads


def multiply(rows_refs, w_ref, loads):
    own_a_ref, other_a_ref, own_late_ref, other_late_ref = rows_refs
    pieces = ((own_a_ref, NEAR), (own_late_ref, LATE), (other_a_ref, NEAR), (other_late_ref, LATE))
    total = jnp.zeros((4 * LIVE, 256), F32)
    for load in loads:
        load.wait()
    for z in range(16):
        rows = jnp.concatenate([ref[z, 0:count, :] for ref, count in pieces], axis=0)
        total = total + jnp.dot(rows, w_ref[z // 4, z % 4], preferred_element_type=F32)
    return total


def sent_kernel(place_ref, own_a_ref, other_a_ref, own_late_ref, other_late_ref, w_hbm, sent_ref, w_ref, sems):
    yl, yh, c = place_ref[0], place_ref[1], place_ref[2]
    loads = fetch(w_hbm, w_ref, sems, 4 * (1 - yl))
    index = lax.broadcasted_iota(jnp.int32, (EXTRA, ROWS), 0)
    for i, a_ref in enumerate((own_a_ref, other_a_ref)):
        for flip_h, square in enumerate(square_rows(a_ref)):
            hi, mid, lo = split3(square)
            left = jnp.where(index == 1, mid, 0.0)
            right = jnp.where(index == 0, hi, jnp.where(index == 1, lo, 0.0))
            sent_ref[yh ^ flip_h, c ^ i, LIVE:, 0:ROWS] = left.astype(BF)
            sent_ref[yh ^ flip_h, c ^ i, LIVE:, ROWS:] = right.astype(BF)
    total = multiply((own_a_ref, other_a_ref, own_late_ref, other_late_ref), w_ref, loads)
    for i in range(2):
        for flip_h in range(2):
            first = (2 * i + flip_h) * LIVE
            sent_ref[yh ^ flip_h, c ^ i, 0:LIVE, :] = total[first : first + LIVE, :].astype(BF)


def own_kernel(
    place_ref, own_a_ref, other_a_ref, own_late_ref, other_late_ref, w_hbm,
    own_ref, square_ref, table_ref, w_ref, sems,
):
    loads = fetch(w_hbm, w_ref, sems, 4 * place_ref[0])
    total = multiply((own_a_ref, other_a_ref, own_late_ref, other_late_ref), w_ref, loads)
    for i, a_ref in enumerate((own_a_ref, other_a_ref)):
        lives = a_ref[0, NEAR:, :].astype(F32)
        for flip_h, square in enumerate(square_rows(a_ref)):
            square_ref[i, flip_h] = jnp.broadcast_to(square, (EXTRA, ROWS))
            table_ref[i, flip_h] = slot_table(lives[2 * flip_h : 2 * flip_h + 1, :ROWS]).astype(BF)
            first = (2 * i + flip_h) * LIVE
            own_ref[i, flip_h] = total[first : first + LIVE, :]


def partial(kernel, name, place, rows, weights, out_shape):
    vmem = pl.BlockSpec(memory_space=pltpu.VMEM)
    return pl.pallas_call(
        kernel,
        in_specs=[pl.BlockSpec(memory_space=pltpu.SMEM)] + [vmem] * 4 + [pl.BlockSpec(memory_space=pl.ANY)],
        out_specs=[vmem] * len(out_shape),
        out_shape=out_shape,
        scratch_shapes=[pltpu.VMEM((4, 4, FEATS, 256), BF), pltpu.SemaphoreType.DMA((4,))],
        compiler_params=pltpu.CompilerParams(vmem_limit_bytes=VMEM_BYTES),
        name=name,
    )(place, *rows, weights)


SENT_SHAPES = [jax.ShapeDtypeStruct((2, 2, BLOCK_ROWS, 256), BF)]
OWN_SHAPES = [
    jax.ShapeDtypeStruct((2, 2, LIVE, 256), F32),
    jax.ShapeDtypeStruct((2, 2, EXTRA, ROWS), F32),
    jax.ShapeDtypeStruct((2, 2, LIVE, ROWS), BF),
]


def finish_kernel(place_ref, own_ref, square_ref, table_ref, other_ref, out_ref):
    yh, c = place_ref[1], place_ref[2]
    for flip_h in range(2):
        for i in range(2):
            sent = other_ref[yh ^ flip_h, c ^ i].astype(F32)
            rows = own_ref[i, flip_h] + sent[0:LIVE, :]
            tail = sent[LIVE:, :]
            square = square_ref[i, flip_h, 0:1, :] + tail[0:1, ROWS:] + tail[1:2, :ROWS] + tail[1:2, ROWS:]
            table = table_ref[i, flip_h]
            inverse = lax.rsqrt(square * (1.0 / D) + 1e-06)
            rows = rows * jnp.sum(table.astype(F32) * inverse, axis=1, keepdims=True)
            gate, up = rows[:, :128], rows[:, 128:]
            hidden = (gate / (1.0 + jnp.exp(-gate)) * up).astype(BF)
            spread = lax.dot_general(table, hidden, (((0,), (0,)), ((), ())), preferred_element_type=F32)
            block = 2 * (yh ^ flip_h) + (c ^ i)
            out_ref[pl.ds(pl.multiple_of(block * ROWS, ROWS), ROWS), :] = spread.astype(BF)


def finish(place, own, square, table, other):
    return pl.pallas_call(
        finish_kernel,
        in_specs=[pl.BlockSpec(memory_space=pltpu.SMEM)] + [pl.BlockSpec(memory_space=pltpu.VMEM)] * 4,
        out_specs=pl.BlockSpec(memory_space=pltpu.VMEM),
        out_shape=jax.ShapeDtypeStruct((4 * ROWS, 128), BF),
        compiler_params=pltpu.CompilerParams(vmem_limit_bytes=VMEM_BYTES),
        name="finish",
    )(place, own, square, table, other)


def partner_groups():
    return [
        [((yl * 4 + x) * 2 + (h ^ (yl & c))) * 2 + c for yl in range(2) for x in range(4)]
        for h in range(2)
        for c in range(2)
    ]


def partner_moves():
    moves = []
    for yl in range(2):
        for yh in range(2):
            for c in range(2):
                moves.append(((yl * 2 + yh) * 2 + c, ((1 - yl) * 2 + (yh ^ c)) * 2 + c))
    return moves


def shards(gate_master, up_master, stream, norm_gain, live_rows):
    swap = [(0, 1), (1, 0)]
    place = jnp.stack([lax.axis_index(name) for name in ("yl", "yh", "c")]).astype(jnp.int32)
    block, early = compact(stream, norm_gain, live_rows)
    early = lax.ppermute(early, "yh", swap)
    gate_master, block = lax.optimization_barrier((gate_master, block))
    weights = pack(gate_master, up_master)
    early, weights = lax.optimization_barrier((early, weights))
    weights = lax.all_to_all(weights, ("yl", "x", "yh", "c"), 0, 0, axis_index_groups=partner_groups())
    own_a = lax.all_gather(join(block, early), ("zh", "zl"), axis=0, tiled=False)
    late = own_a[:, EARLY:LIVE, :]
    own_late = lax.ppermute(late, "yh", swap)
    other_late = lax.ppermute(late, ("yh", "c"), [(0, 3), (1, 2), (2, 1), (3, 0)])
    other_a = lax.ppermute(own_a, "c", swap)
    rows = (own_a, other_a, own_late, other_late)
    (sent,) = partial(sent_kernel, "sent_sums", place, rows, weights, SENT_SHAPES)
    other = lax.ppermute(sent, ("yl", "yh", "c"), partner_moves())
    own, square, table = partial(own_kernel, "own_sums", place, rows, weights, OWN_SHAPES)
    return finish(place, own, square, table, other)


def solution(mesh):
    fine = Mesh(mesh.devices.reshape(4, 4, 2, 4, 2, 2), AXES)
    learner, tp = ("zh", "zl", "yl"), ("yh", "c")
    placed = (
        P("x", learner + tp),
        P("x", learner + tp),
        P(("x",) + tp, learner),
        P(learner),
        P(("x",) + tp),
    )
    return jax.shard_map(shards, mesh=fine, in_specs=placed, out_specs=P("x", learner + tp), check_vma=False)
```

```python
import jax
import jax.numpy as jnp
from jax import lax
from jax.experimental import pallas as pl
from jax.experimental.pallas import tpu as pltpu
from jax.sharding import Mesh, PartitionSpec as P

D = 8192
LIVE = 64
ROWS = 128
FEATS = 256
EXTRA = 8
BLOCK_ROWS = LIVE + EXTRA
EARLY = 56
TAIL = 4
LATE = LIVE - EARLY
NEAR = LIVE + EARLY
AXES = ("zh", "zl", "yl", "x", "yh", "c")
BF = jnp.bfloat16
F32 = jnp.float32
VMEM_BYTES = 24 * 1024 * 1024


def split3(value):
    hi = value.astype(BF).astype(F32)
    mid = (value - hi).astype(BF).astype(F32)
    lo = (value - hi - mid).astype(BF).astype(F32)
    return hi, mid, lo


def diagonal(size):
    return lax.broadcasted_iota(jnp.int32, (size, size), 0) == lax.broadcasted_iota(jnp.int32, (size, size), 1)


def slot_table(live):
    rows = lax.broadcasted_iota(jnp.int32, (ROWS, ROWS), 0)
    cols = lax.broadcasted_iota(jnp.int32, (ROWS, ROWS), 1)
    before = jnp.where(rows <= cols, 1.0, 0.0).astype(BF)
    wide = jnp.broadcast_to(live, (16, ROWS))
    rank = jnp.dot(wide.astype(BF), before, preferred_element_type=F32)[0:1, :]
    slot = lax.broadcasted_iota(jnp.int32, (LIVE, ROWS), 0).astype(F32) + 1.0
    return jnp.where((slot == rank) & (live > 0.5), 1.0, 0.0)


def compact_kernel(stream_ref, gain_ref, live_ref, block_ref, early_ref):
    stream = stream_ref[...]
    live = live_ref[...].astype(F32)
    table = slot_table(live)
    scaled = (stream * gain_ref[...]).astype(BF)
    rows = jnp.dot(table.astype(BF), scaled, preferred_element_type=F32).astype(BF)
    block_ref[0:LIVE, :] = rows
    early_ref[0:EARLY, :] = rows[0:EARLY, :]
    square = jnp.sum(stream * stream, axis=1, keepdims=True)
    square_row = jnp.sum(jnp.where(diagonal(ROWS), square, 0.0), axis=0, keepdims=True)
    hi, mid, lo = split3(square_row)
    index = lax.broadcasted_iota(jnp.int32, (EXTRA, ROWS), 0)
    for ref, start, first in ((block_ref, LIVE, 0), (early_ref, EARLY, 2)):
        ref[start:, 0:ROWS] = jnp.where(index == first, live, jnp.where(index == first + 1, mid, 0.0)).astype(BF)
        ref[start:, ROWS:] = jnp.where(index == first, hi, jnp.where(index == first + 1, lo, 0.0)).astype(BF)


def compact(stream, gain, live):
    return pl.pallas_call(
        compact_kernel,
        out_shape=[
            jax.ShapeDtypeStruct((BLOCK_ROWS, FEATS), BF),
            jax.ShapeDtypeStruct((EARLY + EXTRA, FEATS), BF),
        ],
        name="compact",
    )(stream, gain.reshape(1, FEATS), live.reshape(1, ROWS))


def join(block, early):
    tail = (block[LIVE:] + early[EARLY:])[:TAIL]
    return jnp.concatenate([block[:LIVE], early[:EARLY], tail], axis=0)


def power_below(value):
    wide = value * 8388609.0
    return jnp.abs(wide - wide * (1.0 - 2.0**-24))


def restore(master):
    tile = master.T.reshape(4, 32, 128)
    size = jnp.abs(tile)
    largest = jnp.max(size, axis=1, keepdims=True)
    power = power_below(largest)
    power = jnp.where(power > largest, power * 0.5, power)
    power = jnp.where(power * 2.0 <= largest, power * 2.0, power)
    scale = jnp.clip(power, 2.0**-32, 2.0**4) * 0.25
    inverse = power_below((4.0 / scale) * (1.0 + 2.0**-10))
    quarters = jnp.floor(size * inverse)
    step = jnp.where(quarters < 8.0, 1.5 * 2.0**24, jnp.where(quarters < 16.0, 1.5 * 2.0**25, 1.5 * 2.0**26))
    level = jnp.minimum((quarters + 0.5 + step) - step, 24.0)
    quarter = scale * 0.25
    return (level * jnp.where(tile < 0.0, -quarter, quarter)).reshape(128, 128).T.astype(BF)


def pack_kernel(gate_hbm, up_hbm, out_hbm, gate_ref, up_ref, packed_ref, in_sems, out_sems):
    loads = []
    for zl in range(4):
        rows = pl.ds(zl * 2 * FEATS, 2 * FEATS)
        for side, (hbm, ref) in enumerate(((gate_hbm, gate_ref), (up_hbm, up_ref))):
            load = pltpu.make_async_copy(hbm.at[rows, :], ref.at[rows, :], in_sems.at[zl, side])
            load.start()
            loads.append(load)
    stores = []
    for zl in range(4):
        loads[2 * zl].wait()
        loads[2 * zl + 1].wait()
        for yl in range(2):
            for side, ref in enumerate((gate_ref, up_ref)):
                for tile in range(2):
                    first = (2 * zl + yl) * FEATS + tile * 128
                    value = restore(ref[first : first + 128, :])
                    packed_ref[yl, zl, tile * 128 : (tile + 1) * 128, side * 128 : (side + 1) * 128] = value
            for x in range(4):
                store = pltpu.make_async_copy(packed_ref.at[yl, zl], out_hbm.at[2 * x + yl, zl], out_sems.at[zl, yl, x])
                store.start()
                stores.append(store)
    for store in stores:
        store.wait()


def pack(gate_master, up_master):
    return pl.pallas_call(
        pack_kernel,
        in_specs=[pl.BlockSpec(memory_space=pl.ANY)] * 2,
        out_specs=pl.BlockSpec(memory_space=pl.ANY),
        out_shape=jax.ShapeDtypeStruct((8, 4, FEATS, 256), BF),
        scratch_shapes=[
            pltpu.VMEM((8 * FEATS, 128), F32),
            pltpu.VMEM((8 * FEATS, 128), F32),
            pltpu.VMEM((2, 4, FEATS, 256), BF),
            pltpu.SemaphoreType.DMA((4, 2)),
            pltpu.SemaphoreType.DMA((4, 2, 4)),
        ],
        compiler_params=pltpu.CompilerParams(vmem_limit_bytes=62 * 1024 * 1024),
        name="pack",
    )(gate_master, up_master)


def square_rows(a_ref):
    tails = jnp.sum(a_ref[:, NEAR:, :].astype(F32), axis=0)
    return [tails[t : t + 1, ROWS:] + tails[t + 1 : t + 2, :ROWS] + tails[t + 1 : t + 2, ROWS:] for t in (0, 2)]


def fetch(w_hbm, w_ref, sems, first):
    loads = [pltpu.make_async_copy(w_hbm.at[2 * x + first], w_ref.at[x], sems.at[x]) for x in range(4)]
    for load in loads:
        load.start()
    return loads


def multiply(rows_refs, w_ref, loads):
    own_a_ref, other_a_ref, own_late_ref, other_late_ref = rows_refs
    pieces = ((own_a_ref, NEAR), (own_late_ref, LATE), (other_a_ref, NEAR), (other_late_ref, LATE))
    total = jnp.zeros((4 * LIVE, 256), F32)
    for load in loads:
        load.wait()
    for z in range(16):
        rows = jnp.concatenate([ref[z, 0:count, :] for ref, count in pieces], axis=0)
        total = total + jnp.dot(rows, w_ref[z // 4, z % 4], preferred_element_type=F32)
    return total


def sent_kernel(place_ref, own_a_ref, other_a_ref, own_late_ref, other_late_ref, w_hbm, sent_ref, w_ref, sems):
    yl, yh, c = place_ref[0], place_ref[1], place_ref[2]
    loads = fetch(w_hbm, w_ref, sems, 1 - yl)
    index = lax.broadcasted_iota(jnp.int32, (EXTRA, ROWS), 0)
    for i, a_ref in enumerate((own_a_ref, other_a_ref)):
        for flip_h, square in enumerate(square_rows(a_ref)):
            hi, mid, lo = split3(square)
            left = jnp.where(index == 1, mid, 0.0)
            right = jnp.where(index == 0, hi, jnp.where(index == 1, lo, 0.0))
            sent_ref[yh ^ flip_h, c ^ i, LIVE:, 0:ROWS] = left.astype(BF)
            sent_ref[yh ^ flip_h, c ^ i, LIVE:, ROWS:] = right.astype(BF)
    total = multiply((own_a_ref, other_a_ref, own_late_ref, other_late_ref), w_ref, loads)
    for i in range(2):
        for flip_h in range(2):
            first = (2 * i + flip_h) * LIVE
            sent_ref[yh ^ flip_h, c ^ i, 0:LIVE, :] = total[first : first + LIVE, :].astype(BF)


def own_kernel(
    place_ref, own_a_ref, other_a_ref, own_late_ref, other_late_ref, w_hbm,
    own_ref, square_ref, table_ref, w_ref, sems,
):
    loads = fetch(w_hbm, w_ref, sems, place_ref[0])
    total = multiply((own_a_ref, other_a_ref, own_late_ref, other_late_ref), w_ref, loads)
    for i, a_ref in enumerate((own_a_ref, other_a_ref)):
        lives = a_ref[0, NEAR:, :].astype(F32)
        for flip_h, square in enumerate(square_rows(a_ref)):
            square_ref[i, flip_h] = jnp.broadcast_to(square, (EXTRA, ROWS))
            table_ref[i, flip_h] = slot_table(lives[2 * flip_h : 2 * flip_h + 1, :ROWS]).astype(BF)
            first = (2 * i + flip_h) * LIVE
            own_ref[i, flip_h] = total[first : first + LIVE, :]


def partial(kernel, name, place, rows, weights, out_shape):
    vmem = pl.BlockSpec(memory_space=pltpu.VMEM)
    return pl.pallas_call(
        kernel,
        in_specs=[pl.BlockSpec(memory_space=pltpu.SMEM)] + [vmem] * 4 + [pl.BlockSpec(memory_space=pl.ANY)],
        out_specs=[vmem] * len(out_shape),
        out_shape=out_shape,
        scratch_shapes=[pltpu.VMEM((4, 4, FEATS, 256), BF), pltpu.SemaphoreType.DMA((4,))],
        compiler_params=pltpu.CompilerParams(vmem_limit_bytes=VMEM_BYTES),
        name=name,
    )(place, *rows, weights)


SENT_SHAPES = [jax.ShapeDtypeStruct((2, 2, BLOCK_ROWS, 256), BF)]
OWN_SHAPES = [
    jax.ShapeDtypeStruct((2, 2, LIVE, 256), F32),
    jax.ShapeDtypeStruct((2, 2, EXTRA, ROWS), F32),
    jax.ShapeDtypeStruct((2, 2, LIVE, ROWS), BF),
]


def finish_kernel(place_ref, own_ref, square_ref, table_ref, other_ref, out_ref):
    yh, c = place_ref[1], place_ref[2]
    for flip_h in range(2):
        for i in range(2):
            sent = other_ref[yh ^ flip_h, c ^ i].astype(F32)
            rows = own_ref[i, flip_h] + sent[0:LIVE, :]
            tail = sent[LIVE:, :]
            square = square_ref[i, flip_h, 0:1, :] + tail[0:1, ROWS:] + tail[1:2, :ROWS] + tail[1:2, ROWS:]
            table = table_ref[i, flip_h]
            inverse = lax.rsqrt(square * (1.0 / D) + 1e-06)
            rows = rows * jnp.sum(table.astype(F32) * inverse, axis=1, keepdims=True)
            gate, up = rows[:, :128], rows[:, 128:]
            hidden = (gate / (1.0 + jnp.exp(-gate)) * up).astype(BF)
            spread = lax.dot_general(table, hidden, (((0,), (0,)), ((), ())), preferred_element_type=F32)
            block = 2 * (yh ^ flip_h) + (c ^ i)
            out_ref[pl.ds(pl.multiple_of(block * ROWS, ROWS), ROWS), :] = spread.astype(BF)


def finish(place, own, square, table, other):
    return pl.pallas_call(
        finish_kernel,
        in_specs=[pl.BlockSpec(memory_space=pltpu.SMEM)] + [pl.BlockSpec(memory_space=pltpu.VMEM)] * 4,
        out_specs=pl.BlockSpec(memory_space=pltpu.VMEM),
        out_shape=jax.ShapeDtypeStruct((4 * ROWS, 128), BF),
        compiler_params=pltpu.CompilerParams(vmem_limit_bytes=VMEM_BYTES),
        name="finish",
    )(place, own, square, table, other)


def partner_groups():
    return [
        [((yl * 4 + x) * 2 + (h ^ (yl & c))) * 2 + c for x in range(4) for yl in range(2)]
        for h in range(2)
        for c in range(2)
    ]


def partner_moves():
    moves = []
    for yl in range(2):
        for yh in range(2):
            for c in range(2):
                moves.append(((yl * 2 + yh) * 2 + c, ((1 - yl) * 2 + (yh ^ c)) * 2 + c))
    return moves


def shards(gate_master, up_master, stream, norm_gain, live_rows):
    swap = [(0, 1), (1, 0)]
    place = jnp.stack([lax.axis_index(name) for name in ("yl", "yh", "c")]).astype(jnp.int32)
    block, early = compact(stream, norm_gain, live_rows)
    early = lax.ppermute(early, "yh", swap)
    gate_master, block = lax.optimization_barrier((gate_master, block))
    weights = pack(gate_master, up_master)
    early, weights = lax.optimization_barrier((early, weights))
    weights = lax.all_to_all(weights, ("yl", "x", "yh", "c"), 0, 0, axis_index_groups=partner_groups())
    own_a = lax.all_gather(join(block, early), ("zh", "zl"), axis=0, tiled=False)
    late = own_a[:, EARLY:LIVE, :]
    own_late = lax.ppermute(late, "yh", swap)
    other_late = lax.ppermute(late, ("yh", "c"), [(0, 3), (1, 2), (2, 1), (3, 0)])
    other_a = lax.ppermute(own_a, "c", swap)
    rows = (own_a, other_a, own_late, other_late)
    (sent,) = partial(sent_kernel, "sent_sums", place, rows, weights, SENT_SHAPES)
    other = lax.ppermute(sent, ("yl", "yh", "c"), partner_moves())
    own, square, table = partial(own_kernel, "own_sums", place, rows, weights, OWN_SHAPES)
    return finish(place, own, square, table, other)


def solution(mesh):
    fine = Mesh(mesh.devices.reshape(4, 4, 2, 4, 2, 2), AXES)
    learner, tp = ("zh", "zl", "yl"), ("yh", "c")
    placed = (
        P("x", learner + tp),
        P("x", learner + tp),
        P(("x",) + tp, learner),
        P(learner),
        P(("x",) + tp),
    )
    return jax.shard_map(shards, mesh=fine, in_specs=placed, out_specs=P("x", learner + tp), check_vma=False)
```

```python
import jax
import jax.numpy as jnp
from jax import lax
from jax.experimental import pallas as pl
from jax.experimental.pallas import tpu as pltpu
from jax.sharding import Mesh, PartitionSpec as P

D = 8192
LIVE = 64
ROWS = 128
FEATS = 256
EXTRA = 8
BLOCK_ROWS = LIVE + EXTRA
EARLY = 48
LATE = LIVE - EARLY
NEAR = LIVE + EARLY
AXES = ("zh", "zl", "yl", "x", "yh", "c")
BF = jnp.bfloat16
F32 = jnp.float32
VMEM_BYTES = 24 * 1024 * 1024


def split3(value):
    hi = value.astype(BF).astype(F32)
    mid = (value - hi).astype(BF).astype(F32)
    lo = (value - hi - mid).astype(BF).astype(F32)
    return hi, mid, lo


def diagonal(size):
    return lax.broadcasted_iota(jnp.int32, (size, size), 0) == lax.broadcasted_iota(jnp.int32, (size, size), 1)


def slot_table(live):
    rows = lax.broadcasted_iota(jnp.int32, (ROWS, ROWS), 0)
    cols = lax.broadcasted_iota(jnp.int32, (ROWS, ROWS), 1)
    before = jnp.where(rows <= cols, 1.0, 0.0).astype(BF)
    wide = jnp.broadcast_to(live, (16, ROWS))
    rank = jnp.dot(wide.astype(BF), before, preferred_element_type=F32)[0:1, :]
    slot = lax.broadcasted_iota(jnp.int32, (LIVE, ROWS), 0).astype(F32) + 1.0
    return jnp.where((slot == rank) & (live > 0.5), 1.0, 0.0)


def compact_kernel(stream_hbm, gain_hbm, live_hbm, block_ref, early_ref, stream_ref, gain_ref, live_ref, sems):
    pairs = ((live_hbm, live_ref), (gain_hbm, gain_ref), (stream_hbm, stream_ref))
    loads = [pltpu.make_async_copy(hbm, ref, sems.at[i]) for i, (hbm, ref) in enumerate(pairs)]
    for load in loads:
        load.start()
    loads[0].wait()
    live = live_ref[...].astype(F32)
    table = slot_table(live)
    loads[1].wait()
    loads[2].wait()
    stream = stream_ref[...]
    scaled = (stream * gain_ref[...]).astype(BF)
    rows = jnp.dot(table.astype(BF), scaled, preferred_element_type=F32).astype(BF)
    block_ref[0:LIVE, :] = rows
    early_ref[0:EARLY, :] = rows[0:EARLY, :]
    square = jnp.sum(stream * stream, axis=1, keepdims=True)
    square_row = jnp.sum(jnp.where(diagonal(ROWS), square, 0.0), axis=0, keepdims=True)
    hi, mid, lo = split3(square_row)
    index = lax.broadcasted_iota(jnp.int32, (EXTRA, ROWS), 0)
    for ref, start, first in ((block_ref, LIVE, 0), (early_ref, EARLY, 2)):
        ref[start:, 0:ROWS] = jnp.where(index == first, live, jnp.where(index == first + 1, mid, 0.0)).astype(BF)
        ref[start:, ROWS:] = jnp.where(index == first, hi, jnp.where(index == first + 1, lo, 0.0)).astype(BF)


def compact(stream, gain, live):
    return pl.pallas_call(
        compact_kernel,
        in_specs=[pl.BlockSpec(memory_space=pl.ANY)] * 3,
        out_specs=[pl.BlockSpec(memory_space=pltpu.VMEM)] * 2,
        scratch_shapes=[
            pltpu.VMEM((ROWS, FEATS), F32),
            pltpu.VMEM((1, FEATS), F32),
            pltpu.VMEM((1, ROWS), jnp.int32),
            pltpu.SemaphoreType.DMA((3,)),
        ],
        out_shape=[
            jax.ShapeDtypeStruct((BLOCK_ROWS, FEATS), BF),
            jax.ShapeDtypeStruct((EARLY + EXTRA, FEATS), BF),
        ],
        compiler_params=pltpu.CompilerParams(vmem_limit_bytes=62 * 1024 * 1024),
        name="compact",
    )(stream, gain.reshape(1, FEATS), live.reshape(1, ROWS))


def join(block, early):
    return jnp.concatenate([block[:LIVE], early[:EARLY], block[LIVE:] + early[EARLY:]], axis=0)


def power_below(value):
    wide = value * 8388609.0
    return jnp.abs(wide - wide * (1.0 - 2.0**-24))


def restore(master):
    tile = master.T.reshape(4, 32, 128)
    size = jnp.abs(tile)
    largest = jnp.max(size, axis=1, keepdims=True)
    power = power_below(largest)
    power = jnp.where(power > largest, power * 0.5, power)
    power = jnp.where(power * 2.0 <= largest, power * 2.0, power)
    scale = jnp.clip(power, 2.0**-32, 2.0**4) * 0.25
    inverse = power_below((4.0 / scale) * (1.0 + 2.0**-10))
    quarters = jnp.floor(size * inverse)
    step = jnp.where(quarters < 8.0, 1.5 * 2.0**24, jnp.where(quarters < 16.0, 1.5 * 2.0**25, 1.5 * 2.0**26))
    level = jnp.minimum((quarters + 0.5 + step) - step, 24.0)
    quarter = scale * 0.25
    return (level * jnp.where(tile < 0.0, -quarter, quarter)).reshape(128, 128).T.astype(BF)


def pack_kernel(gate_hbm, up_hbm, out_hbm, gate_ref, up_ref, packed_ref, in_sems, out_sems):
    loads = []
    for zl in range(4):
        rows = pl.ds(zl * 2 * FEATS, 2 * FEATS)
        for side, (hbm, ref) in enumerate(((gate_hbm, gate_ref), (up_hbm, up_ref))):
            load = pltpu.make_async_copy(hbm.at[rows, :], ref.at[rows, :], in_sems.at[zl, side])
            load.start()
            loads.append(load)
    stores = []
    for zl in range(4):
        loads[2 * zl].wait()
        loads[2 * zl + 1].wait()
        for yl in range(2):
            for side, ref in enumerate((gate_ref, up_ref)):
                for tile in range(2):
                    first = (2 * zl + yl) * FEATS + tile * 128
                    value = restore(ref[first : first + 128, :])
                    packed_ref[yl, zl, tile * 128 : (tile + 1) * 128, side * 128 : (side + 1) * 128] = value
            for x in range(4):
                store = pltpu.make_async_copy(packed_ref.at[yl, zl], out_hbm.at[2 * x + yl, zl], out_sems.at[zl, yl, x])
                store.start()
                stores.append(store)
    for store in stores:
        store.wait()


def pack(gate_master, up_master):
    return pl.pallas_call(
        pack_kernel,
        in_specs=[pl.BlockSpec(memory_space=pl.ANY)] * 2,
        out_specs=pl.BlockSpec(memory_space=pl.ANY),
        out_shape=jax.ShapeDtypeStruct((8, 4, FEATS, 256), BF),
        scratch_shapes=[
            pltpu.VMEM((8 * FEATS, 128), F32),
            pltpu.VMEM((8 * FEATS, 128), F32),
            pltpu.VMEM((2, 4, FEATS, 256), BF),
            pltpu.SemaphoreType.DMA((4, 2)),
            pltpu.SemaphoreType.DMA((4, 2, 4)),
        ],
        compiler_params=pltpu.CompilerParams(vmem_limit_bytes=62 * 1024 * 1024),
        name="pack",
    )(gate_master, up_master)


def square_rows(a_ref):
    tails = jnp.sum(a_ref[:, NEAR:, :].astype(F32), axis=0)
    return [tails[t : t + 1, ROWS:] + tails[t + 1 : t + 2, :ROWS] + tails[t + 1 : t + 2, ROWS:] for t in (0, 2)]


def fetch(w_hbm, w_ref, sems, first):
    loads = [pltpu.make_async_copy(w_hbm.at[2 * x + first], w_ref.at[x], sems.at[x]) for x in range(4)]
    for load in loads:
        load.start()
    return loads


def multiply(rows_refs, w_ref, loads):
    own_a_ref, other_a_ref, own_late_ref, other_late_ref = rows_refs
    pieces = ((own_a_ref, NEAR), (own_late_ref, LATE), (other_a_ref, NEAR), (other_late_ref, LATE))
    total = jnp.zeros((4 * LIVE, 256), F32)
    for load in loads:
        load.wait()
    for z in range(16):
        rows = jnp.concatenate([ref[z, 0:count, :] for ref, count in pieces], axis=0)
        total = total + jnp.dot(rows, w_ref[z // 4, z % 4], preferred_element_type=F32)
    return total


def sent_kernel(place_ref, own_a_ref, other_a_ref, own_late_ref, other_late_ref, w_hbm, sent_ref, w_ref, sems):
    yl, yh, c = place_ref[0], place_ref[1], place_ref[2]
    loads = fetch(w_hbm, w_ref, sems, 1 - yl)
    index = lax.broadcasted_iota(jnp.int32, (EXTRA, ROWS), 0)
    for i, a_ref in enumerate((own_a_ref, other_a_ref)):
        for flip_h, square in enumerate(square_rows(a_ref)):
            hi, mid, lo = split3(square)
            left = jnp.where(index == 1, mid, 0.0)
            right = jnp.where(index == 0, hi, jnp.where(index == 1, lo, 0.0))
            sent_ref[yh ^ flip_h, c ^ i, LIVE:, 0:ROWS] = left.astype(BF)
            sent_ref[yh ^ flip_h, c ^ i, LIVE:, ROWS:] = right.astype(BF)
    total = multiply((own_a_ref, other_a_ref, own_late_ref, other_late_ref), w_ref, loads)
    for i in range(2):
        for flip_h in range(2):
            first = (2 * i + flip_h) * LIVE
            sent_ref[yh ^ flip_h, c ^ i, 0:LIVE, :] = total[first : first + LIVE, :].astype(BF)


def own_kernel(
    place_ref, own_a_ref, other_a_ref, own_late_ref, other_late_ref, w_hbm,
    own_ref, square_ref, table_ref, w_ref, sems,
):
    loads = fetch(w_hbm, w_ref, sems, place_ref[0])
    total = multiply((own_a_ref, other_a_ref, own_late_ref, other_late_ref), w_ref, loads)
    for i, a_ref in enumerate((own_a_ref, other_a_ref)):
        lives = a_ref[0, NEAR:, :].astype(F32)
        for flip_h, square in enumerate(square_rows(a_ref)):
            square_ref[i, flip_h] = jnp.broadcast_to(square, (EXTRA, ROWS))
            table_ref[i, flip_h] = slot_table(lives[2 * flip_h : 2 * flip_h + 1, :ROWS]).astype(BF)
            first = (2 * i + flip_h) * LIVE
            own_ref[i, flip_h] = total[first : first + LIVE, :]


def partial(kernel, name, place, rows, weights, out_shape):
    vmem = pl.BlockSpec(memory_space=pltpu.VMEM)
    return pl.pallas_call(
        kernel,
        in_specs=[pl.BlockSpec(memory_space=pltpu.SMEM)] + [vmem] * 4 + [pl.BlockSpec(memory_space=pl.ANY)],
        out_specs=[vmem] * len(out_shape),
        out_shape=out_shape,
        scratch_shapes=[pltpu.VMEM((4, 4, FEATS, 256), BF), pltpu.SemaphoreType.DMA((4,))],
        compiler_params=pltpu.CompilerParams(vmem_limit_bytes=VMEM_BYTES),
        name=name,
    )(place, *rows, weights)


SENT_SHAPES = [jax.ShapeDtypeStruct((2, 2, BLOCK_ROWS, 256), BF)]
OWN_SHAPES = [
    jax.ShapeDtypeStruct((2, 2, LIVE, 256), F32),
    jax.ShapeDtypeStruct((2, 2, EXTRA, ROWS), F32),
    jax.ShapeDtypeStruct((2, 2, LIVE, ROWS), BF),
]


def finish_kernel(place_ref, own_ref, square_ref, table_ref, other_ref, out_ref):
    yh, c = place_ref[1], place_ref[2]
    for flip_h in range(2):
        for i in range(2):
            sent = other_ref[yh ^ flip_h, c ^ i].astype(F32)
            rows = own_ref[i, flip_h] + sent[0:LIVE, :]
            tail = sent[LIVE:, :]
            square = square_ref[i, flip_h, 0:1, :] + tail[0:1, ROWS:] + tail[1:2, :ROWS] + tail[1:2, ROWS:]
            table = table_ref[i, flip_h]
            inverse = lax.rsqrt(square * (1.0 / D) + 1e-06)
            rows = rows * jnp.sum(table.astype(F32) * inverse, axis=1, keepdims=True)
            gate, up = rows[:, :128], rows[:, 128:]
            hidden = (gate / (1.0 + jnp.exp(-gate)) * up).astype(BF)
            spread = lax.dot_general(table, hidden, (((0,), (0,)), ((), ())), preferred_element_type=F32)
            block = 2 * (yh ^ flip_h) + (c ^ i)
            out_ref[pl.ds(pl.multiple_of(block * ROWS, ROWS), ROWS), :] = spread.astype(BF)


def finish(place, own, square, table, other):
    return pl.pallas_call(
        finish_kernel,
        in_specs=[pl.BlockSpec(memory_space=pltpu.SMEM)] + [pl.BlockSpec(memory_space=pltpu.VMEM)] * 4,
        out_specs=pl.BlockSpec(memory_space=pltpu.VMEM),
        out_shape=jax.ShapeDtypeStruct((4 * ROWS, 128), BF),
        compiler_params=pltpu.CompilerParams(vmem_limit_bytes=VMEM_BYTES),
        name="finish",
    )(place, own, square, table, other)


def partner_groups():
    return [
        [((yl * 4 + x) * 2 + (h ^ (yl & c))) * 2 + c for x in range(4) for yl in range(2)]
        for h in range(2)
        for c in range(2)
    ]


def partner_moves():
    moves = []
    for yl in range(2):
        for yh in range(2):
            for c in range(2):
                moves.append(((yl * 2 + yh) * 2 + c, ((1 - yl) * 2 + (yh ^ c)) * 2 + c))
    return moves


def shards(gate_master, up_master, stream, norm_gain, live_rows):
    swap = [(0, 1), (1, 0)]
    place = jnp.stack([lax.axis_index(name) for name in ("yl", "yh", "c")]).astype(jnp.int32)
    block, early = compact(stream, norm_gain, live_rows)
    early = lax.ppermute(early, "yh", swap)
    gate_master, block = lax.optimization_barrier((gate_master, block))
    weights = pack(gate_master, up_master)
    early, weights = lax.optimization_barrier((early, weights))
    weights = lax.all_to_all(weights, ("yl", "x", "yh", "c"), 0, 0, axis_index_groups=partner_groups())
    own_a = lax.all_gather(join(block, early), ("zh", "zl"), axis=0, tiled=False)
    late = own_a[:, EARLY:LIVE, :]
    own_late = lax.ppermute(late, "yh", swap)
    other_late = lax.ppermute(late, ("yh", "c"), [(0, 3), (1, 2), (2, 1), (3, 0)])
    other_a = lax.ppermute(own_a, "c", swap)
    rows = (own_a, other_a, own_late, other_late)
    (sent,) = partial(sent_kernel, "sent_sums", place, rows, weights, SENT_SHAPES)
    other = lax.ppermute(sent, ("yl", "yh", "c"), partner_moves())
    own, square, table = partial(own_kernel, "own_sums", place, rows, weights, OWN_SHAPES)
    return finish(place, own, square, table, other)


def solution(mesh):
    fine = Mesh(mesh.devices.reshape(4, 4, 2, 4, 2, 2), AXES)
    learner, tp = ("zh", "zl", "yl"), ("yh", "c")
    placed = (
        P("x", learner + tp),
        P("x", learner + tp),
        P(("x",) + tp, learner),
        P(learner),
        P(("x",) + tp),
    )
    return jax.shard_map(shards, mesh=fine, in_specs=placed, out_specs=P("x", learner + tp), check_vma=False)
```
